256 devices in a mesh: dp: 8 (over x, y_hi), fsdp: 32 (over y_lo, z, core).
Axes of the slice: x: 4, y: 4 (y_hi: 2, y_lo: 2; y = y_hi * 2 + y_lo), z: 8, core: 2. Of those that a mesh axis runs over, the one named last changes fastest.
Arguments:
- hidden: bfloat16 [65536, 5120], P(('dp', 'fsdp')), may hold values from -6 to 6
- queries: bfloat16 [65536, 2560], P(('dp', 'fsdp')), may hold values from -64 to 64
- upstream: bfloat16 [65536, 2560], P(('dp', 'fsdp')), may hold values from -6 to 6
- segment_ids: int32 [256, 256], P(('dp', 'fsdp')), may hold values from 0 to 3, never falling along the last dimension, each value on 1 to 128 neighbouring positions
- prompt_lengths: int32 [256, 4], P(('dp', 'fsdp')), may hold values from 1 to 128
- advantages: float32 [256, 4], P(('dp', 'fsdp')), may hold values from -16 to 16
- kv_weight: bfloat16 [5120, 1024], P('fsdp'), may hold values from -0.078125 to 0.078125
- master: float32 [5120, 1024], P('fsdp', 'dp'), may hold values from -3 to 3
- moment_one: float32 [5120, 1024], P('fsdp', 'dp'), may hold values from -0.03 to 0.03
- moment_two: float32 [5120, 1024], P('fsdp', 'dp'), may hold values from 1e-06 to 0.0001
Outputs:
- query_grad: bfloat16 [65536, 2560], P(('dp', 'fsdp'))
- hidden_grad: bfloat16 [65536, 5120], P(('dp', 'fsdp'))
- new_master: float32 [5120, 1024], P('fsdp', 'dp')
- new_moment_one: float32 [5120, 1024], P('fsdp', 'dp')
- new_moment_two: float32 [5120, 1024], P('fsdp', 'dp')
The draws below stay inside these ranges and needn't reach their ends.
Inputs may be any that keep to these rules, and one draw needn't show every extreme that they name: `segment_ids`: in each row ids never fall, each rollout has 1 to 128 tokens and some rollout has exactly 128.
All inputs are finite; a program needn't handle non-finite values.
Results may differ from the reference program's by a relative error of at most 0.035.
The reference program's roundings to bfloat16 on the way (of `keys`, `probs_low`, `grad_out`, `grad_scores` and `kv_grad`) count: a program that leaves them out, or rounds other values in their place, can miss the bound.
Values may be sent and summed in bfloat16 or wider, within the bound.
No kernel may reach another device: no remote copies, remote signals or barrier semaphores. Data moves between devices by JAX's collectives and lax.ppermute only.
A program may use at most 128 MiB of HBM per device.

```python
import math
import jax
import jax.numpy as jnp
import numpy as np
from jax import lax

D = 5120
HD = 128
QW = 2560
KVW = 1024
TOK_DEV = 256
SEGS = 4
MOST = 128
PROMPT_MOST = 128
STEP = 10
ROWS = 256
TOKENS = 65536


def draw_queries(key, part):
    key = jax.random.fold_in(key, 11)
    entries = jax.random.normal(key, (TOKENS, QW), jnp.float32)
    return jnp.clip(entries, -6.0, 6.0).astype(jnp.bfloat16)


def draw_prompt_lengths(key, part):
    key = jax.random.fold_in(key, 23)
    row_index = jnp.arange(ROWS, dtype=jnp.int32)
    span = jnp.maximum(ROWS - 1, 1)
    ceiling = PROMPT_MOST - (PROMPT_MOST - 1) * row_index // span
    ceiling = jnp.maximum(ceiling, 1)
    upper = jnp.broadcast_to(ceiling[:, None] + 1, (ROWS, SEGS))
    drawn = jax.random.randint(key, (ROWS, SEGS), jnp.ones((ROWS, SEGS), jnp.int32), upper, dtype=jnp.int32)
    return drawn.at[0, 0].set(PROMPT_MOST)


def draw_advantages(key, part):
    key = jax.random.fold_in(key, 37)
    row_index = jnp.arange(ROWS, dtype=jnp.float32)
    span = jnp.float32(max(ROWS - 1, 1))
    row_scale = 0.25 * jnp.exp(row_index / span * math.log(16.0))
    entries = jnp.clip(jax.random.normal(key, (ROWS, SEGS), jnp.float32), -3.5, 3.5)
    return jnp.clip(entries * row_scale[:, None], -16.0, 16.0)


def block_levels(own_key, dims, pieces, low, high):
    factor_of = 1.0
    for dim, parts in pieces:
        steps = jax.random.uniform(jax.random.fold_in(jax.random.fold_in(own_key, 6), dim), (parts,), jnp.float32, low / len(pieces), high / len(pieces))
        factor_of = factor_of * jnp.repeat(jnp.exp(steps), dims[dim] // parts).reshape((-1,) + (1,) * (len(dims) - 1 - dim))
    return factor_of


def length_profile(amount, total, most, lean):
    portions = [(1 << 20) // math.isqrt(rank ** lean) + 1 for rank in range(2, amount + 1)]
    surplus, counts = total - most - (amount - 1), [1] * (amount - 1)
    while surplus > 0:
        movable = [i for i in range(amount - 1) if counts[i] < most]
        mass, budget = sum([portions[i] for i in movable]), surplus
        for i in movable:
            more = min(most - counts[i], max(1, budget * portions[i] // mass), surplus)
            counts[i] = counts[i] + more
            surplus = surplus - more
    return np.array([most] + counts)


def ragged_sizes(stream_key, amount, total, most, lean):
    if amount == 2:
        one = jax.random.randint(stream_key, (), max(1, total - most), min(most, total - 1) + 1)
        return jnp.stack([one, total - one])
    tallies = jnp.asarray(length_profile(amount, total, most, lean), jnp.int32)
    pairs = (amount - 1) // 2
    donor, sink = tallies[1:1 + 2 * pairs:2], tallies[2:2 + 2 * pairs:2]
    margin = jnp.minimum(donor - 1, most - sink)
    shifted = jax.random.randint(jax.random.fold_in(stream_key, 1), (pairs,), 0, 1 << 20) % (margin + 1)
    tallies = tallies.at[1:1 + 2 * pairs:2].set(donor - shifted).at[2:2 + 2 * pairs:2].set(sink + shifted)
    return tallies[jax.random.permutation(jax.random.fold_in(stream_key, 2), amount)]


def scatter_about(key, extent, deviation, most, cuts=(), kind=jnp.bfloat16):
    factor_of = block_levels(key, extent, cuts, -0.22, 0.18) if cuts else 1.0
    values = jax.random.normal(key, extent, jnp.float32) * deviation * factor_of
    return jnp.minimum(jnp.maximum(values, -most), most).astype(kind)


def setup_inputs(seed: int = 0) -> dict:
    splits = jax.random.split(jax.random.key(seed), 11)
    hidden = scatter_about(splits[0], (TOKENS, D), 1.0, 6.0, ((0, 256),))
    queries = draw_queries(jax.random.fold_in(splits[10], 71), 0)
    upstream = scatter_about(splits[2], (TOKENS, QW), 1.0, 6.0, ((0, 256),))
    segment_ids = jax.vmap(lambda own: jnp.searchsorted(jnp.cumsum(ragged_sizes(own, SEGS, TOK_DEV, MOST, 2)), jnp.arange(TOK_DEV), side="right"))(jax.random.split(splits[3], ROWS)).reshape((ROWS, TOK_DEV)).astype(jnp.int32)
    prompt_lengths = draw_prompt_lengths(jax.random.fold_in(splits[10], 71), 0)
    advantages = draw_advantages(jax.random.fold_in(splits[10], 71), 0)
    kv_weight = scatter_about(splits[6], (D, KVW), D ** -0.5, 0.078125, ((0, 32),))
    master = scatter_about(splits[7], (D, KVW), 0.5, 3.0, ((0, 32), (1, 8)), jnp.float32)
    moment_one = scatter_about(splits[8], (D, KVW), 0.004, 0.03, ((0, 32), (1, 8)), jnp.float32)
    moment_two = jnp.clip(jnp.exp(math.log(0.0001) - 4.6051702 * jax.random.uniform(splits[9], (D, KVW), jnp.float32) ** block_levels(splits[9], (D, KVW), ((0, 32), (1, 8)), -0.2, 0.2)), 9.999999974752427e-07, 0.0001)
    return {"hidden": hidden, "queries": queries, "upstream": upstream, "segment_ids": segment_ids, "prompt_lengths": prompt_lengths, "advantages": advantages, "kv_weight": kv_weight, "master": master, "moment_one": moment_one, "moment_two": moment_two}


ROPE_BASE = 1000000.0

def positions_in_row(segs):
    length = segs.shape[0]
    index = jnp.arange(length, dtype=jnp.int32)
    previous = jnp.concatenate([segs[:1] - 1, segs[:-1]])
    starts = jnp.where(segs != previous, index, jnp.zeros_like(index))
    return index - lax.cummax(starts)

def token_terms(segs, prompts, advs):
    pos = positions_in_row(segs)
    onehot = segs[:, None] == jnp.arange(prompts.shape[0], dtype=jnp.int32)[None, :]
    prompt_tok = lax.optimization_barrier(jnp.sum(jnp.where(onehot, prompts[None, :], jnp.zeros_like(prompts)[None, :]), axis=1))
    adv_tok = lax.optimization_barrier(jnp.sum(jnp.where(onehot, advs[None, :], jnp.zeros_like(advs)[None, :]), axis=1))
    return (pos, pos >= prompt_tok, adv_tok)

def rotate(values):
    half = values.shape[-1] // 2
    return jnp.concatenate([-values[..., half:], values[..., :half]], axis=-1)

def attention_backward(kv_pre, queries, upstream, segs, pos, weight):
    length = segs.shape[0]
    kv_half = kv_pre.shape[1] // 2
    head_size = HD
    heads = kv_half // head_size
    group = queries.shape[1] // kv_half
    freq = ROPE_BASE ** (-(jnp.arange(head_size // 2, dtype=jnp.float32) * 2.0 / head_size))
    angle = pos.astype(jnp.float32)[:, None] * freq[None, :]
    cosine = jnp.concatenate([jnp.cos(angle), jnp.cos(angle)], axis=1)[:, None, :]
    sine = jnp.concatenate([jnp.sin(angle), jnp.sin(angle)], axis=1)[:, None, :]
    keys_pre = kv_pre[:, :kv_half].reshape(length, heads, head_size)
    keys = (keys_pre * cosine + rotate(keys_pre) * sine).astype(jnp.bfloat16)
    values = kv_pre[:, kv_half:].reshape(length, heads, head_size).astype(jnp.bfloat16)
    query_heads = queries.reshape(length, heads, group, head_size)
    scale = 1.0 / jnp.sqrt(jnp.float32(head_size))
    scores = jnp.einsum('qkgd,tkd->kgqt', query_heads.astype(jnp.float32), keys.astype(jnp.float32)) * scale
    index = jnp.arange(length, dtype=jnp.int32)
    allowed = (segs[:, None] == segs[None, :]) & (index[None, :] <= index[:, None])
    scores = jnp.where(allowed[None, None], scores, jnp.float32(-1e+30))
    probs = jax.nn.softmax(scores, axis=-1)
    probs_low = probs.astype(jnp.bfloat16)
    output = jnp.einsum('kgqt,tkd->qkgd', probs_low.astype(jnp.float32), values.astype(jnp.float32))
    grad_out = (upstream.astype(jnp.float32) * weight[:, None]).astype(jnp.bfloat16).reshape(length, heads, group, head_size)
    delta = jnp.einsum('qkgd,qkgd->kgq', grad_out.astype(jnp.float32), output)
    grad_probs = jnp.einsum('qkgd,tkd->kgqt', grad_out.astype(jnp.float32), values.astype(jnp.float32))
    grad_scores = (probs * (grad_probs - delta[..., None])).astype(jnp.bfloat16)
    query_grad = (jnp.einsum('kgqt,tkd->qkgd', grad_scores.astype(jnp.float32), keys.astype(jnp.float32)) * scale).astype(jnp.bfloat16)
    key_grad = jnp.einsum('kgqt,qkgd->tkd', grad_scores.astype(jnp.float32), query_heads.astype(jnp.float32)) * scale
    value_grad = jnp.einsum('kgqt,qkgd->tkd', probs_low.astype(jnp.float32), grad_out.astype(jnp.float32))
    key_grad_pre = key_grad * cosine - rotate(key_grad * sine)
    kv_grad = jnp.concatenate([key_grad_pre.reshape(length, kv_half), value_grad.reshape(length, kv_half)], axis=1).astype(jnp.bfloat16)
    return (query_grad.reshape(length, queries.shape[1]), kv_grad)

def reference(hidden, queries, upstream, segment_ids, prompt_lengths, advantages, kv_weight, master, moment_one, moment_two):
    rows, length = segment_ids.shape
    pos_all, live_all, adv_all = jax.vmap(token_terms)(segment_ids, prompt_lengths, advantages)
    count = jnp.sum(live_all.astype(jnp.float32))
    factor = jnp.float32(TOKENS) / jnp.maximum(count, jnp.float32(1.0))
    weight_all = jnp.where(live_all, adv_all * factor, jnp.zeros_like(adv_all))
    hidden_rows = hidden.reshape(rows, length, hidden.shape[1])
    query_rows = queries.reshape(rows, length, queries.shape[1])
    upstream_rows = upstream.reshape(rows, length, upstream.shape[1])

    def one_row(total, items):
        x_row, q_row, u_row, segs, pos, weight = items
        kv_pre = jnp.dot(x_row, kv_weight, preferred_element_type=jnp.float32)
        query_grad, kv_grad = attention_backward(kv_pre, q_row, u_row, segs, pos, weight)
        hidden_grad = lax.dot_general(kv_grad, kv_weight, (((1,), (1,)), ((), ())), preferred_element_type=jnp.float32).astype(jnp.bfloat16)
        term = lax.dot_general(x_row, kv_grad, (((0,), (0,)), ((), ())), preferred_element_type=jnp.float32)
        total = total + lax.optimization_barrier(term.astype(jnp.bfloat16)).astype(jnp.float32)
        return (total, (query_grad, hidden_grad))
    start = jnp.zeros(kv_weight.shape, jnp.float32)
    total, (query_grad, hidden_grad) = lax.scan(one_row, start, (hidden_rows, query_rows, upstream_rows, segment_ids, pos_all, weight_all))
    weight_grad = total / jnp.float32(TOKENS)
    new_moment_one = 0.9 * moment_one + 0.1 * weight_grad
    new_moment_two = 0.999 * moment_two + 0.001 * weight_grad * weight_grad
    first_hat = new_moment_one / (1.0 - 0.9 ** STEP)
    second_hat = new_moment_two / (1.0 - 0.999 ** STEP)
    new_master = master - 0.001 * (first_hat / (jnp.sqrt(second_hat) + 1e-08) + 0.1 * master)
    return (query_grad.reshape(queries.shape), hidden_grad.reshape(hidden.shape), new_master, new_moment_one, new_moment_two)
```

```python
import jax
import jax.numpy as jnp
from jax import lax
from jax.experimental import pallas as pl
from jax.experimental.pallas import tpu as pltpu
from jax.sharding import Mesh, PartitionSpec as P

HD = 128
STEP = 10
ROPE_BASE = 1000000.0
GROUP = 5
KVH = 4
SCALE = HD**-0.5
RZ = 64
RA = 48
Y = ("yh", "yl")
F32 = jnp.float32
BF16 = jnp.bfloat16


def positions_in_row(segs):
    length = segs.shape[0]
    index = jnp.arange(length, dtype=jnp.int32)
    previous = jnp.concatenate([segs[:1] - 1, segs[:-1]])
    starts = jnp.where(segs != previous, index, jnp.zeros_like(index))
    return index - lax.cummax(starts)


def token_terms(segs, prompts, advs):
    pos = positions_in_row(segs)
    onehot = segs[:, None] == jnp.arange(prompts.shape[0], dtype=jnp.int32)[None, :]
    prompt_tok = jnp.sum(
        jnp.where(onehot, prompts[None, :], jnp.zeros_like(prompts)[None, :]), axis=1
    )
    adv_tok = jnp.sum(jnp.where(onehot, advs[None, :], jnp.zeros_like(advs)[None, :]), axis=1)
    return (pos, pos >= prompt_tok, adv_tok)


def shift(v, axis, n, k):
    return lax.ppermute(v, axis, [(i, (i + k) % n) for i in range(n)])


def swap(v, axis, n, bit):
    return lax.ppermute(v, axis, [(i, i ^ bit) for i in range(n)])


def total_of(v):
    for axis, n, bit in (
        ("c", 2, 1), ("x", 4, 1), ("x", 4, 2), ("yl", 2, 1), ("yh", 2, 1),
        ("z", 8, 1), ("z", 8, 2), ("z", 8, 4),
    ):
        v = v + swap(v, axis, n, bit)
    return v


def dot_nt(a, b):
    return lax.dot_general(a, b, (((1,), (1,)), ((), ())), preferred_element_type=F32)


def dot_tn(a, b):
    return lax.dot_general(a, b, (((0,), (0,)), ((), ())), preferred_element_type=F32)


def attention_kernel(kpre, vpre, q, up, cos, sin, start, weight, qg, kvg):
    length = kpre.shape[0]
    cosine, sine = cos[...], sin[...]
    kp = kpre[...]
    k = (kp * cosine + pltpu.roll(kp, HD // 2, 1) * sine).astype(BF16)
    v = vpre[...].astype(BF16)
    key_index = lax.broadcasted_iota(jnp.int32, (length, length), 0)
    query_index = lax.broadcasted_iota(jnp.int32, (length, length), 1)
    allowed = (key_index >= start[...]) & (key_index <= query_index)
    w = weight[...]
    dk = jnp.zeros((length, HD), F32)
    dv = jnp.zeros((length, HD), F32)
    for g in range(GROUP):
        cols = slice(g * HD, (g + 1) * HD)
        qh = q[:, cols]
        do = (up[:, cols].astype(F32) * w).astype(BF16)
        s = jnp.where(allowed, dot_nt(k, qh) * SCALE, F32(-1e30))
        e = jnp.exp(s - jnp.max(s, axis=0, keepdims=True))
        p = e * (1.0 / jnp.sum(e, axis=0, keepdims=True))
        low = p.astype(BF16)
        dp = dot_nt(v, do)
        delta = jnp.sum(low.astype(F32) * dp, axis=0, keepdims=True)
        ds = (p * (dp - delta)).astype(BF16)
        qg[:, cols] = (dot_tn(ds, k) * SCALE).astype(BF16)
        dk = dk + jnp.dot(ds, qh, preferred_element_type=F32)
        dv = dv + jnp.dot(low, do, preferred_element_type=F32)
    dk = dk * SCALE
    kvg[0] = (dk * cosine - pltpu.roll(dk, HD // 2, 1) * sine).astype(BF16)
    kvg[1] = dv.astype(BF16)


def attention_backward(kv_pre, queries, upstream, pos, weight):
    length = pos.shape[0]
    freq = ROPE_BASE ** (-(jnp.arange(HD // 2, dtype=F32) * 2.0 / HD))
    angle = pos.astype(F32)[:, None] * freq[None, :]
    cosine = jnp.concatenate([jnp.cos(angle), jnp.cos(angle)], axis=1)
    sine = jnp.concatenate([-jnp.sin(angle), jnp.sin(angle)], axis=1)
    start = (jnp.arange(length, dtype=jnp.int32) - pos)[None, :]
    whole = lambda shape: pl.BlockSpec(shape, lambda h: (0, 0))
    return pl.pallas_call(
        attention_kernel,
        grid=(KVH,),
        in_specs=[
            pl.BlockSpec((length, HD), lambda h: (0, h)),
            pl.BlockSpec((length, HD), lambda h: (0, h + KVH)),
            pl.BlockSpec((length, GROUP * HD), lambda h: (0, h)),
            pl.BlockSpec((length, GROUP * HD), lambda h: (0, h)),
            whole((length, HD)),
            whole((length, HD)),
            whole((1, length)),
            whole((length, 1)),
        ],
        out_specs=[
            pl.BlockSpec((length, GROUP * HD), lambda h: (0, h)),
            pl.BlockSpec((2, length, HD), lambda h: (0, 0, h)),
        ],
        out_shape=[
            jax.ShapeDtypeStruct((length, KVH * GROUP * HD), BF16),
            jax.ShapeDtypeStruct((2, length, KVH * HD), BF16),
        ],
        compiler_params=pltpu.CompilerParams(vmem_limit_bytes=32 * 2**20),
    )(kv_pre, kv_pre, queries, upstream, cosine, sine, start, weight[:, None])


def pick(v, index, axis):
    return lax.dynamic_index_in_dim(v, index, axis, keepdims=False)


def add_up(parts):
    total = parts[0].astype(F32)
    for part in parts[1:]:
        total = total + part.astype(F32)
    return total


def body(
    hidden,
    queries,
    upstream,
    segment_ids,
    prompt_lengths,
    advantages,
    kv_weight,
    master,
    moment_one,
    moment_two,
):
    barrier = lax.optimization_barrier
    x, z, c = lax.axis_index("x"), lax.axis_index("z"), lax.axis_index("c")
    y = lax.axis_index(Y)
    length, width = hidden.shape
    rows = kv_weight.shape[0]
    cols = kv_weight.shape[1]
    segs = segment_ids[0]
    full_weight = lax.all_gather(kv_weight, ("yl", "z", "c"), axis=0, tiled=True)
    pos, live, adv_tok = token_terms(segs, prompt_lengths[0], advantages[0])
    local_count = jnp.sum(live.astype(F32))
    count = total_of(jnp.broadcast_to(local_count, (8, 128)))[0, 0]
    total_tokens = length * 256
    factor = F32(total_tokens) / jnp.maximum(count, F32(1.0))
    weight = jnp.where(live, adv_tok * factor, jnp.zeros_like(adv_tok))

    hidden_t = hidden.T.reshape(16, 2, rows, length)
    mine = pick(hidden_t, c, 1)
    theirs = shift(pick(hidden_t, 1 - c, 1), "c", 2, 1)
    hidden_pair = jnp.concatenate([mine, theirs], axis=-1).reshape(2, 8, rows, 2 * length)
    hz = jnp.transpose(hidden_pair[:, :, :RZ], (1, 0, 2, 3)).reshape(16 * RZ, 2 * length)
    ha = hidden_pair[:, :, RZ : RZ + RA].reshape(16 * RA, 2 * length)
    hb = hidden_pair[:, :, RZ + RA :].reshape(2, 8 * RA, 2 * length)

    kv_pre = jnp.dot(hidden, full_weight, preferred_element_type=F32)
    query_grad, kv_grad = attention_backward(kv_pre, queries, upstream, pos, weight)
    kv_sib = shift(kv_grad, "c", 2, 1)
    pair = jnp.concatenate([kv_grad, kv_sib], axis=1)
    pair = jnp.concatenate([pair[0], pair[1]], axis=1)

    part_z = jnp.dot(hz, pair, preferred_element_type=F32).astype(BF16)
    sum_z = lax.psum_scatter(part_z, "z", scatter_dimension=0, tiled=True)

    def to_x(k):
        cols = lax.dynamic_slice_in_dim(pair, lax.rem(x + k, 4) * 2 * HD, 2 * HD, axis=1)
        return jnp.dot(ha, cols, preferred_element_type=F32).astype(BF16)

    def to_y(k):
        there = lax.rem(y + k, 4)
        cols = pick(pair.reshape(2 * length, 4, 2, HD), there // 2, 2).reshape(2 * length, 4 * HD)
        return jnp.dot(pick(hb, lax.rem(there, 2), 0), cols, preferred_element_type=F32).astype(BF16)

    def block_y(v, k):
        there = lax.rem(y + k, 4)
        v = v.reshape(2, -1, 2 * HD)
        at = (lax.rem(there, 2), 0, there // 2 * HD)
        return lax.dynamic_slice(v, at, (1, v.shape[1], HD))[0]

    def block_x(v, k, width):
        return lax.dynamic_slice_in_dim(v, lax.rem(x + k, 4) * width, width, axis=1)

    a_out = [to_x(k) for k in (0, 1, 2, 3)]
    b_out = [to_y(k) for k in (0, 1, 2, 3)]
    arrived = barrier(
        tuple(shift(a_out[k], "x", 4, k) for k in (1, 2, 3))
        + tuple(shift(b_out[k], Y, 4, k) for k in (1, 2, 3))
    )
    a = add_up([a_out[0], *arrived[:3]]).astype(BF16)
    b = add_up([b_out[0], *arrived[3:]]).astype(BF16)
    arrived = barrier(
        tuple(shift(block_y(a, k), Y, 4, k) for k in (1, 2, 3))
        + tuple(shift(block_x(b, k, HD), "x", 4, k) for k in (1, 2, 3))
    )
    a = add_up([block_y(a, 0), *arrived[:3]]).reshape(8, RA, HD)
    b = add_up([block_x(b, 0, HD), *arrived[3:]]).reshape(8, RA, HD)
    ab = jnp.concatenate([a, b], axis=1).astype(BF16)
    ab_parts = barrier(
        tuple(shift(pick(ab, lax.rem(z + k, 8), 0), "z", 8, k) for k in (4, 3, 5, 2, 6, 1, 7))
    )
    ab_sum = add_up([pick(ab, z, 0), *ab_parts])

    parts = barrier(tuple(shift(block_x(sum_z, k, 2 * HD), "x", 4, k) for k in (1, 2, 3)))
    s = add_up([block_x(sum_z, 0, 2 * HD), *parts]).astype(BF16)
    parts = barrier(tuple(shift(block_y(s, k), Y, 4, k) for k in (1, 2, 3)))
    s = add_up([block_y(s, 0), *parts])
    summed = jnp.concatenate([s, ab_sum], axis=0)

    hidden_grad = dot_nt(kv_grad[0], full_weight[:, : KVH * HD]) + dot_nt(
        kv_grad[1], full_weight[:, KVH * HD :]
    )
    weight_grad = summed / F32(total_tokens)
    new_moment_one = 0.9 * moment_one + 0.1 * weight_grad
    new_moment_two = 0.999 * moment_two + 0.001 * weight_grad * weight_grad
    first_hat = new_moment_one / (1.0 - 0.9**STEP)
    second_hat = new_moment_two / (1.0 - 0.999**STEP)
    new_master = master - 0.001 * (first_hat / (jnp.sqrt(second_hat) + 1e-08) + 0.1 * master)
    return (
        query_grad,
        hidden_grad.astype(BF16),
        new_master,
        new_moment_one,
        new_moment_two,
    )


def solution(mesh):
    names = ("x", "yh", "yl", "z", "c")
    fine = Mesh(mesh.devices.reshape(4, 2, 2, 8, 2), names)
    tokens = P(names, None)
    state = P(("yl", "z", "c"), ("x", "yh"))
    return jax.shard_map(
        body,
        mesh=fine,
        in_specs=(tokens,) * 6 + (P(("yl", "z", "c"), None), state, state, state),
        out_specs=(tokens, tokens, state, state, state),
        check_vma=False,
    )
```

```python
import jax
import jax.numpy as jnp
from jax import lax
from jax.experimental import pallas as pl
from jax.experimental.pallas import tpu as pltpu
from jax.sharding import Mesh, PartitionSpec as P

HD = 128
STEP = 10
ROPE_BASE = 1000000.0
GROUP = 5
KVH = 4
SCALE = HD**-0.5
RZ = 64
RA = 48
Y = ("yh", "yl")
F32 = jnp.float32
BF16 = jnp.bfloat16


def positions_in_row(segs):
    length = segs.shape[0]
    index = jnp.arange(length, dtype=jnp.int32)
    previous = jnp.concatenate([segs[:1] - 1, segs[:-1]])
    starts = jnp.where(segs != previous, index, jnp.zeros_like(index))
    return index - lax.cummax(starts)


def token_terms(segs, prompts, advs):
    pos = positions_in_row(segs)
    onehot = segs[:, None] == jnp.arange(prompts.shape[0], dtype=jnp.int32)[None, :]
    prompt_tok = jnp.sum(
        jnp.where(onehot, prompts[None, :], jnp.zeros_like(prompts)[None, :]), axis=1
    )
    adv_tok = jnp.sum(jnp.where(onehot, advs[None, :], jnp.zeros_like(advs)[None, :]), axis=1)
    return (pos, pos >= prompt_tok, adv_tok)


def shift(v, axis, n, k):
    return lax.ppermute(v, axis, [(i, (i + k) % n) for i in range(n)])


def swap(v, axis, n, bit):
    return lax.ppermute(v, axis, [(i, i ^ bit) for i in range(n)])


def total_of(v):
    for axis, n, bit in (
        ("c", 2, 1), ("x", 4, 1), ("x", 4, 2), ("yl", 2, 1), ("yh", 2, 1),
        ("z", 8, 1), ("z", 8, 2), ("z", 8, 4),
    ):
        v = v + swap(v, axis, n, bit)
    return v


def dot_nt(a, b):
    return lax.dot_general(a, b, (((1,), (1,)), ((), ())), preferred_element_type=F32)


def dot_tn(a, b):
    return lax.dot_general(a, b, (((0,), (0,)), ((), ())), preferred_element_type=F32)


def attention_kernel(hidden, wk, wv, q, up, cos, sin, start, weight, qg, kvg):
    length = hidden.shape[0]
    cosine, sine = cos[...], sin[...]
    both = jnp.concatenate([wk[...], wv[...]], axis=1)
    pre = jnp.dot(hidden[...], both, preferred_element_type=F32)
    kp = pre[:, :HD]
    k = (kp * cosine + pltpu.roll(kp, HD // 2, 1) * sine).astype(BF16)
    v = pre[:, HD:].astype(BF16)
    key_index = lax.broadcasted_iota(jnp.int32, (length, length), 0)
    query_index = lax.broadcasted_iota(jnp.int32, (length, length), 1)
    allowed = (key_index >= start[...]) & (key_index <= query_index)
    w = weight[...]
    dk = jnp.zeros((length, HD), F32)
    dv = jnp.zeros((length, HD), F32)
    for g in range(GROUP):
        cols = slice(g * HD, (g + 1) * HD)
        qh = q[:, cols]
        do = (up[:, cols].astype(F32) * w).astype(BF16)
        s = jnp.where(allowed, dot_nt(k, qh) * SCALE, F32(-1e30))
        e = jnp.exp(s - jnp.max(s, axis=0, keepdims=True))
        p = e * (1.0 / jnp.sum(e, axis=0, keepdims=True))
        low = p.astype(BF16)
        dp = dot_nt(v, do)
        delta = jnp.sum(low.astype(F32) * dp, axis=0, keepdims=True)
        ds = (p * (dp - delta)).astype(BF16)
        qg[:, cols] = (dot_tn(ds, k) * SCALE).astype(BF16)
        dk = dk + jnp.dot(ds, qh, preferred_element_type=F32)
        dv = dv + jnp.dot(low, do, preferred_element_type=F32)
    dk = dk * SCALE
    at = pl.multiple_of(pl.program_id(0) * HD, HD)
    kvg[:, pl.ds(at, HD)] = (dk * cosine - pltpu.roll(dk, HD // 2, 1) * sine).astype(BF16)
    kvg[:, pl.ds(at + KVH * HD, HD)] = dv.astype(BF16)


def attention_backward(hidden, full_weight, queries, upstream, pos, weight):
    length = pos.shape[0]
    freq = ROPE_BASE ** (-(jnp.arange(HD // 2, dtype=F32) * 2.0 / HD))
    angle = pos.astype(F32)[:, None] * freq[None, :]
    cosine = jnp.concatenate([jnp.cos(angle), jnp.cos(angle)], axis=1)
    sine = jnp.concatenate([-jnp.sin(angle), jnp.sin(angle)], axis=1)
    start = (jnp.arange(length, dtype=jnp.int32) - pos)[None, :]
    whole = lambda shape: pl.BlockSpec(shape, lambda h: (0, 0))
    return pl.pallas_call(
        attention_kernel,
        grid=(KVH,),
        in_specs=[
            whole(hidden.shape),
            pl.BlockSpec((hidden.shape[1], HD), lambda h: (0, h)),
            pl.BlockSpec((hidden.shape[1], HD), lambda h: (0, h + KVH)),
            pl.BlockSpec((length, GROUP * HD), lambda h: (0, h)),
            pl.BlockSpec((length, GROUP * HD), lambda h: (0, h)),
            whole((length, HD)),
            whole((length, HD)),
            whole((1, length)),
            whole((length, 1)),
        ],
        out_specs=[
            pl.BlockSpec((length, GROUP * HD), lambda h: (0, h)),
            whole((length, 2 * KVH * HD)),
        ],
        out_shape=[
            jax.ShapeDtypeStruct((length, KVH * GROUP * HD), BF16),
            jax.ShapeDtypeStruct((length, 2 * KVH * HD), BF16),
        ],
        compiler_params=pltpu.CompilerParams(vmem_limit_bytes=32 * 2**20),
    )(hidden, full_weight, full_weight, queries, upstream, cosine, sine, start, weight[:, None])


def hidden_grad_kernel(kv, w, out):
    out[...] = dot_nt(kv[...], w[...]).astype(BF16)


def hidden_gradient(kv_grad, full_weight):
    length, cols = kv_grad.shape
    width = full_weight.shape[0]
    block = width // 8
    return pl.pallas_call(
        hidden_grad_kernel,
        grid=(8,),
        in_specs=[
            pl.BlockSpec((length, cols), lambda i: (0, 0)),
            pl.BlockSpec((block, cols), lambda i: (i, 0)),
        ],
        out_specs=pl.BlockSpec((length, block), lambda i: (0, i)),
        out_shape=jax.ShapeDtypeStruct((length, width), BF16),
        compiler_params=pltpu.CompilerParams(vmem_limit_bytes=24 * 2**20),
    )(kv_grad, full_weight)


def terms_kernel(place, ha, hb, pair, *refs):
    a_out, b_out, by_yh = refs[:4], refs[4:8], refs[8]
    for yh in range(2):
        for x in range(4):
            block = (2 * x + yh) * HD
            by_yh[yh, :, x * HD : (x + 1) * HD] = pair[:, block : block + HD]
    for k in range(4):
        at = pl.multiple_of(lax.rem(place[0] + k, 4) * 2 * HD, 2 * HD)
        cols = pair[:, pl.ds(at, 2 * HD)]
        a_out[k][...] = jnp.dot(ha[...], cols, preferred_element_type=F32).astype(BF16)
    for k in range(4):
        there = lax.rem(place[1] + k, 4)
        yl, yh = lax.rem(there, 2), lax.div(there, 2)
        b_out[k][...] = jnp.dot(hb[yl], by_yh[yh], preferred_element_type=F32).astype(BF16)


VMEM = pl.BlockSpec(memory_space=pltpu.VMEM)
SMEM = pl.BlockSpec(memory_space=pltpu.SMEM)


def terms(place, ha, hb, pair):
    a_shape = jax.ShapeDtypeStruct((ha.shape[0], 2 * HD), BF16)
    b_shape = jax.ShapeDtypeStruct((hb.shape[1], 4 * HD), BF16)
    return pl.pallas_call(
        terms_kernel,
        in_specs=[SMEM, VMEM, VMEM, VMEM],
        out_specs=[VMEM] * 8,
        out_shape=[a_shape] * 4 + [b_shape] * 4,
        scratch_shapes=[pltpu.VMEM((2, pair.shape[0], 4 * HD), BF16)],
        compiler_params=pltpu.CompilerParams(vmem_limit_bytes=24 * 2**20),
    )(place, ha, hb, pair)


def turn_kernel(place, *refs):
    a_in, b_in, a_out, b_out, a_sum, b_sum = refs[:4], refs[4:8], refs[8:12], refs[12:16], *refs[16:]
    a_sum[...] = add_up([r[...] for r in a_in]).astype(BF16)
    b_sum[...] = add_up([r[...] for r in b_in]).astype(BF16)
    half = a_sum.shape[0] // 2
    for k in range(4):
        there = lax.rem(place[1] + k, 4)
        row = pl.multiple_of(lax.rem(there, 2) * half, half)
        col = pl.multiple_of(lax.div(there, 2) * HD, HD)
        a_out[k][...] = a_sum[pl.ds(row, half), pl.ds(col, HD)]
        col = pl.multiple_of(lax.rem(place[0] + k, 4) * HD, HD)
        b_out[k][...] = b_sum[:, pl.ds(col, HD)]


def turn(place, a_in, b_in):
    rows = b_in[0].shape[0]
    shape = jax.ShapeDtypeStruct((rows, HD), BF16)
    return pl.pallas_call(
        turn_kernel,
        in_specs=[SMEM] + [VMEM] * 8,
        out_specs=[VMEM] * 8,
        out_shape=[shape] * 8,
        scratch_shapes=[pltpu.VMEM(a_in[0].shape, BF16), pltpu.VMEM(b_in[0].shape, BF16)],
        compiler_params=pltpu.CompilerParams(vmem_limit_bytes=24 * 2**20),
    )(place, *a_in, *b_in)


def pick(v, index, axis):
    return lax.dynamic_index_in_dim(v, index, axis, keepdims=False)


def add_up(parts):
    total = parts[0].astype(F32)
    for part in parts[1:]:
        total = total + part.astype(F32)
    return total


def body(
    hidden,
    queries,
    upstream,
    segment_ids,
    prompt_lengths,
    advantages,
    kv_weight,
    master,
    moment_one,
    moment_two,
):
    barrier = lax.optimization_barrier
    x, z, c = lax.axis_index("x"), lax.axis_index("z"), lax.axis_index("c")
    y = lax.axis_index(Y)
    length, width = hidden.shape
    rows = kv_weight.shape[0]
    cols = kv_weight.shape[1]
    segs = segment_ids[0]
    full_weight = lax.all_gather(kv_weight, ("yl", "z", "c"), axis=0, tiled=True)
    pos, live, adv_tok = token_terms(segs, prompt_lengths[0], advantages[0])
    local_count = jnp.sum(live.astype(F32))
    count = total_of(jnp.broadcast_to(local_count, (8, 128)))[0, 0]
    total_tokens = length * 256
    factor = F32(total_tokens) / jnp.maximum(count, F32(1.0))
    weight = jnp.where(live, adv_tok * factor, jnp.zeros_like(adv_tok))

    hidden_t = hidden.T.reshape(16, 2, rows, length)
    mine = pick(hidden_t, c, 1)
    theirs = shift(pick(hidden_t, 1 - c, 1), "c", 2, 1)
    hidden_pair = jnp.concatenate([mine, theirs], axis=-1).reshape(2, 8, rows, 2 * length)
    hz = jnp.transpose(hidden_pair[:, :, :RZ], (1, 0, 2, 3)).reshape(16 * RZ, 2 * length)
    ha = hidden_pair[:, :, RZ : RZ + RA].reshape(16 * RA, 2 * length)
    hb = hidden_pair[:, :, RZ + RA :].reshape(2, 8 * RA, 2 * length)

    hidden, hz, ha, hb = barrier((hidden, hz, ha, hb))

    query_grad, kv_grad = attention_backward(hidden, full_weight, queries, upstream, pos, weight)
    pair = jnp.concatenate([kv_grad, shift(kv_grad, "c", 2, 1)], axis=0)

    part_z = jnp.dot(hz, pair, preferred_element_type=F32).astype(BF16)
    sum_z = lax.psum_scatter(part_z, "z", scatter_dimension=0, tiled=True)

    place = jnp.stack([x, y])

    def block_y(v, k):
        there = lax.rem(y + k, 4)
        v = v.reshape(2, -1, 2 * HD)
        at = (lax.rem(there, 2), 0, there // 2 * HD)
        return lax.dynamic_slice(v, at, (1, v.shape[1], HD))[0]

    def block_x(v, k, width):
        return lax.dynamic_slice_in_dim(v, lax.rem(x + k, 4) * width, width, axis=1)

    out = barrier(tuple(terms(place, ha, hb, pair)) + (kv_grad,))
    sent = tuple(shift(out[k], "x", 4, k) for k in (1, 2, 3))
    sent += tuple(shift(out[4 + k], Y, 4, k) for k in (1, 2, 3))
    hidden_grad = hidden_gradient(out[8], full_weight)
    arrived = barrier(sent + (hidden_grad,))
    hidden_grad = arrived[6]
    out = turn(place, (out[0], *arrived[:3]), (out[4], *arrived[3:6]))
    arrived = barrier(
        tuple(shift(out[k], Y, 4, k) for k in (1, 2, 3))
        + tuple(shift(out[4 + k], "x", 4, k) for k in (1, 2, 3))
    )
    a = add_up([out[0], *arrived[:3]]).reshape(8, RA, HD)
    b = add_up([out[4], *arrived[3:]]).reshape(8, RA, HD)
    ab = jnp.concatenate([a, b], axis=1).astype(BF16).reshape(2, 4, 2 * RA, HD)

    ab, sum_z = barrier((ab, sum_z))
    arrived = barrier(
        (swap(pick(ab, 1 - z // 4, 0), "z", 8, 4),)
        + tuple(shift(block_x(sum_z, k, 2 * HD), "x", 4, k) for k in (1, 2, 3))
    )
    ab = add_up([pick(ab, z // 4, 0), arrived[0]]).astype(BF16)
    s = add_up([block_x(sum_z, 0, 2 * HD), *arrived[1:]]).astype(BF16)
    arrived = barrier(
        tuple(swap(pick(ab, lax.rem(z, 4) ^ k, 0), "z", 8, k) for k in (1, 2, 3))
        + tuple(shift(block_y(s, k), Y, 4, k) for k in (1, 2, 3))
    )
    ab = add_up([pick(ab, lax.rem(z, 4), 0), *arrived[:3]])
    s = add_up([block_y(s, 0), *arrived[3:]])
    summed = jnp.concatenate([s, ab], axis=0)
    weight_grad = summed / F32(total_tokens)
    new_moment_one = 0.9 * moment_one + 0.1 * weight_grad
    new_moment_two = 0.999 * moment_two + 0.001 * weight_grad * weight_grad
    first_hat = new_moment_one / (1.0 - 0.9**STEP)
    second_hat = new_moment_two / (1.0 - 0.999**STEP)
    new_master = master - 0.001 * (first_hat / (jnp.sqrt(second_hat) + 1e-08) + 0.1 * master)
    return (
        query_grad,
        hidden_grad,
        new_master,
        new_moment_one,
        new_moment_two,
    )


def solution(mesh):
    names = ("x", "yh", "yl", "z", "c")
    fine = Mesh(mesh.devices.reshape(4, 2, 2, 8, 2), names)
    tokens = P(names, None)
    state = P(("yl", "z", "c"), ("x", "yh"))
    return jax.shard_map(
        body,
        mesh=fine,
        in_specs=(tokens,) * 6 + (P(("yl", "z", "c"), None), state, state, state),
        out_specs=(tokens, tokens, state, state, state),
        check_vma=False,
    )
```

```python
import jax
import jax.numpy as jnp
from jax import lax
from jax.experimental import pallas as pl
from jax.experimental.pallas import tpu as pltpu
from jax.sharding import Mesh, PartitionSpec as P

HD = 128
STEP = 10
ROPE_BASE = 1000000.0
GROUP = 5
KVH = 4
SCALE = HD**-0.5
RZ = 80
RA = 40
Y = ("yh", "yl")
F32 = jnp.float32
BF16 = jnp.bfloat16


def positions_in_row(segs):
    length = segs.shape[0]
    index = jnp.arange(length, dtype=jnp.int32)
    previous = jnp.concatenate([segs[:1] - 1, segs[:-1]])
    starts = jnp.where(segs != previous, index, jnp.zeros_like(index))
    return index - lax.cummax(starts)


def token_terms(segs, prompts, advs):
    pos = positions_in_row(segs)
    onehot = segs[:, None] == jnp.arange(prompts.shape[0], dtype=jnp.int32)[None, :]
    prompt_tok = jnp.sum(
        jnp.where(onehot, prompts[None, :], jnp.zeros_like(prompts)[None, :]), axis=1
    )
    adv_tok = jnp.sum(jnp.where(onehot, advs[None, :], jnp.zeros_like(advs)[None, :]), axis=1)
    return (pos, pos >= prompt_tok, adv_tok)


def shift(v, axis, n, k):
    return lax.ppermute(v, axis, [(i, (i + k) % n) for i in range(n)])


def swap(v, axis, n, bit):
    return lax.ppermute(v, axis, [(i, i ^ bit) for i in range(n)])


def total_of(v):
    for axis, n, bit in (
        ("c", 2, 1), ("x", 4, 1), ("x", 4, 2), ("yl", 2, 1), ("yh", 2, 1),
        ("z", 8, 1), ("z", 8, 2), ("z", 8, 4),
    ):
        v = v + swap(v, axis, n, bit)
    return v


def dot_nt(a, b):
    return lax.dot_general(a, b, (((1,), (1,)), ((), ())), preferred_element_type=F32)


def dot_tn(a, b):
    return lax.dot_general(a, b, (((0,), (0,)), ((), ())), preferred_element_type=F32)


def attention_kernel(kpre, vpre, q, up, cos, sin, start, weight, qg, kvg):
    length = kpre.shape[0]
    cosine, sine = cos[...], sin[...]
    kp = kpre[...]
    k = (kp * cosine + pltpu.roll(kp, HD // 2, 1) * sine).astype(BF16)
    v = vpre[...].astype(BF16)
    key_index = lax.broadcasted_iota(jnp.int32, (length, length), 0)
    query_index = lax.broadcasted_iota(jnp.int32, (length, length), 1)
    allowed = (key_index >= start[...]) & (key_index <= query_index)
    w = weight[...]
    dk = jnp.zeros((length, HD), F32)
    dv = jnp.zeros((length, HD), F32)
    for g in range(GROUP):
        cols = slice(g * HD, (g + 1) * HD)
        qh = q[:, cols]
        do = (up[:, cols].astype(F32) * w).astype(BF16)
        s = jnp.where(allowed, dot_nt(k, qh) * SCALE, F32(-1e30))
        e = jnp.exp(s - jnp.max(s, axis=0, keepdims=True))
        p = e * (1.0 / jnp.sum(e, axis=0, keepdims=True))
        low = p.astype(BF16)
        dp = dot_nt(v, do)
        delta = jnp.sum(low.astype(F32) * dp, axis=0, keepdims=True)
        ds = (p * (dp - delta)).astype(BF16)
        qg[:, cols] = (dot_tn(ds, k) * SCALE).astype(BF16)
        dk = dk + jnp.dot(ds, qh, preferred_element_type=F32)
        dv = dv + jnp.dot(low, do, preferred_element_type=F32)
    dk = dk * SCALE
    at = pl.multiple_of(pl.program_id(0) * HD, HD)
    kvg[:, pl.ds(at, HD)] = (dk * cosine - pltpu.roll(dk, HD // 2, 1) * sine).astype(BF16)
    kvg[:, pl.ds(at + KVH * HD, HD)] = dv.astype(BF16)


def attention_backward(kv_pre, queries, upstream, pos, weight):
    length = pos.shape[0]
    freq = ROPE_BASE ** (-(jnp.arange(HD // 2, dtype=F32) * 2.0 / HD))
    angle = pos.astype(F32)[:, None] * freq[None, :]
    cosine = jnp.concatenate([jnp.cos(angle), jnp.cos(angle)], axis=1)
    sine = jnp.concatenate([-jnp.sin(angle), jnp.sin(angle)], axis=1)
    start = (jnp.arange(length, dtype=jnp.int32) - pos)[None, :]
    whole = lambda shape: pl.BlockSpec(shape, lambda h: (0, 0))
    return pl.pallas_call(
        attention_kernel,
        grid=(KVH,),
        in_specs=[
            pl.BlockSpec((length, HD), lambda h: (0, h)),
            pl.BlockSpec((length, HD), lambda h: (0, h + KVH)),
            pl.BlockSpec((length, GROUP * HD), lambda h: (0, h)),
            pl.BlockSpec((length, GROUP * HD), lambda h: (0, h)),
            whole((length, HD)),
            whole((length, HD)),
            whole((1, length)),
            whole((length, 1)),
        ],
        out_specs=[
            pl.BlockSpec((length, GROUP * HD), lambda h: (0, h)),
            whole((length, 2 * KVH * HD)),
        ],
        out_shape=[
            jax.ShapeDtypeStruct((length, KVH * GROUP * HD), BF16),
            jax.ShapeDtypeStruct((length, 2 * KVH * HD), BF16),
        ],
        compiler_params=pltpu.CompilerParams(vmem_limit_bytes=32 * 2**20),
    )(kv_pre, kv_pre, queries, upstream, cosine, sine, start, weight[:, None])


def hidden_grad_kernel(kv, w, out):
    out[...] = dot_nt(kv[...], w[...]).astype(BF16)


def hidden_gradient(kv_grad, full_weight):
    length, cols = kv_grad.shape
    width = full_weight.shape[0]
    block = width // 8
    return pl.pallas_call(
        hidden_grad_kernel,
        grid=(8,),
        in_specs=[
            pl.BlockSpec((length, cols), lambda i: (0, 0)),
            pl.BlockSpec((block, cols), lambda i: (i, 0)),
        ],
        out_specs=pl.BlockSpec((length, block), lambda i: (0, i)),
        out_shape=jax.ShapeDtypeStruct((length, width), BF16),
        compiler_params=pltpu.CompilerParams(vmem_limit_bytes=48 * 2**20),
    )(kv_grad, full_weight)


def terms_kernel(place, ha, hb, pair, *refs):
    a_out, b_out, by_yh = refs[:4], refs[4:8], refs[8]
    for yh in range(2):
        for x in range(4):
            block = (2 * x + yh) * HD
            by_yh[yh, :, x * HD : (x + 1) * HD] = pair[:, block : block + HD]
    for k in range(4):
        at = pl.multiple_of(lax.rem(place[0] + k, 4) * 2 * HD, 2 * HD)
        cols = pair[:, pl.ds(at, 2 * HD)]
        a_out[k][...] = jnp.dot(ha[...], cols, preferred_element_type=F32).astype(BF16)
    for k in range(4):
        there = lax.rem(place[1] + k, 4)
        yl, yh = lax.rem(there, 2), lax.div(there, 2)
        b_out[k][...] = jnp.dot(hb[yl], by_yh[yh], preferred_element_type=F32).astype(BF16)


VMEM = pl.BlockSpec(memory_space=pltpu.VMEM)
SMEM = pl.BlockSpec(memory_space=pltpu.SMEM)


def terms(place, ha, hb, pair):
    a_shape = jax.ShapeDtypeStruct((ha.shape[0], 2 * HD), BF16)
    b_shape = jax.ShapeDtypeStruct((hb.shape[1], 4 * HD), BF16)
    return pl.pallas_call(
        terms_kernel,
        in_specs=[SMEM, VMEM, VMEM, VMEM],
        out_specs=[VMEM] * 8,
        out_shape=[a_shape] * 4 + [b_shape] * 4,
        scratch_shapes=[pltpu.VMEM((2, pair.shape[0], 4 * HD), BF16)],
        compiler_params=pltpu.CompilerParams(vmem_limit_bytes=24 * 2**20),
    )(place, ha, hb, pair)


def turn_kernel(place, *refs):
    a_in, b_in, a_out, b_out, a_sum, b_sum = refs[:4], refs[4:8], refs[8:12], refs[12:16], *refs[16:]
    a_sum[...] = add_up([r[...] for r in a_in]).astype(BF16)
    b_sum[...] = add_up([r[...] for r in b_in]).astype(BF16)
    half = a_sum.shape[0] // 2
    for k in range(4):
        there = lax.rem(place[1] + k, 4)
        row = pl.multiple_of(lax.rem(there, 2) * half, half)
        col = pl.multiple_of(lax.div(there, 2) * HD, HD)
        a_out[k][...] = a_sum[pl.ds(row, half), pl.ds(col, HD)]
        col = pl.multiple_of(lax.rem(place[0] + k, 4) * HD, HD)
        b_out[k][...] = b_sum[:, pl.ds(col, HD)]


def turn(place, a_in, b_in):
    rows = b_in[0].shape[0]
    shape = jax.ShapeDtypeStruct((rows, HD), BF16)
    return pl.pallas_call(
        turn_kernel,
        in_specs=[SMEM] + [VMEM] * 8,
        out_specs=[VMEM] * 8,
        out_shape=[shape] * 8,
        scratch_shapes=[pltpu.VMEM(a_in[0].shape, BF16), pltpu.VMEM(b_in[0].shape, BF16)],
        compiler_params=pltpu.CompilerParams(vmem_limit_bytes=24 * 2**20),
    )(place, *a_in, *b_in)


def pick(v, index, axis):
    return lax.dynamic_index_in_dim(v, index, axis, keepdims=False)


def add_up(parts):
    total = parts[0].astype(F32)
    for part in parts[1:]:
        total = total + part.astype(F32)
    return total


def body(
    hidden,
    queries,
    upstream,
    segment_ids,
    prompt_lengths,
    advantages,
    kv_weight,
    master,
    moment_one,
    moment_two,
):
    barrier = lax.optimization_barrier
    x, z, c = lax.axis_index("x"), lax.axis_index("z"), lax.axis_index("c")
    y = lax.axis_index(Y)
    length, width = hidden.shape
    rows = kv_weight.shape[0]
    cols = kv_weight.shape[1]
    segs = segment_ids[0]
    full_weight = lax.all_gather(kv_weight, ("yl", "z", "c"), axis=0, tiled=True)
    pos, live, adv_tok = token_terms(segs, prompt_lengths[0], advantages[0])
    local_count = jnp.sum(live.astype(F32))
    count = total_of(jnp.broadcast_to(local_count, (8, 128)))[0, 0]
    total_tokens = length * 256
    factor = F32(total_tokens) / jnp.maximum(count, F32(1.0))
    weight = jnp.where(live, adv_tok * factor, jnp.zeros_like(adv_tok))

    hidden_t = hidden.T.reshape(16, 2, rows, length)
    mine = pick(hidden_t, c, 1)
    theirs = shift(pick(hidden_t, 1 - c, 1), "c", 2, 1)
    hidden_pair = jnp.concatenate([mine, theirs], axis=-1).reshape(2, 8, rows, 2 * length)
    hz = jnp.transpose(hidden_pair[:, :, :RZ], (1, 0, 2, 3)).reshape(16 * RZ, 2 * length)
    ha = hidden_pair[:, :, RZ : RZ + RA].reshape(16 * RA, 2 * length)
    hb = hidden_pair[:, :, RZ + RA :].reshape(2, 8 * RA, 2 * length)

    hidden, hz, ha, hb = barrier((hidden, hz, ha, hb))

    kv_pre = jnp.dot(hidden, full_weight, preferred_element_type=F32)
    query_grad, kv_grad = attention_backward(kv_pre, queries, upstream, pos, weight)
    pair = jnp.concatenate([kv_grad, shift(kv_grad, "c", 2, 1)], axis=0)

    part_z = jnp.dot(hz, pair, preferred_element_type=F32).astype(BF16)
    sum_z = lax.psum_scatter(part_z, "z", scatter_dimension=0, tiled=True)

    place = jnp.stack([x, y])

    def block_y(v, k):
        there = lax.rem(y + k, 4)
        v = v.reshape(2, -1, 2 * HD)
        at = (lax.rem(there, 2), 0, there // 2 * HD)
        return lax.dynamic_slice(v, at, (1, v.shape[1], HD))[0]

    def block_x(v, k, width):
        return lax.dynamic_slice_in_dim(v, lax.rem(x + k, 4) * width, width, axis=1)

    out = barrier(tuple(terms(place, ha, hb, pair)) + (kv_grad,))
    sent = tuple(shift(out[k], "x", 4, k) for k in (1, 2, 3))
    sent += tuple(shift(out[4 + k], Y, 4, k) for k in (1, 2, 3))
    hidden_grad = hidden_gradient(out[8], full_weight)
    arrived = barrier(sent + (hidden_grad,))
    hidden_grad = arrived[6]
    out = turn(place, (out[0], *arrived[:3]), (out[4], *arrived[3:6]))
    arrived = barrier(
        tuple(shift(out[k], Y, 4, k) for k in (1, 2, 3))
        + tuple(shift(out[4 + k], "x", 4, k) for k in (1, 2, 3))
    )
    a = add_up([out[0], *arrived[:3]]).reshape(8, RA, HD)
    b = add_up([out[4], *arrived[3:]]).reshape(8, RA, HD)
    ab = jnp.concatenate([a, b], axis=1).astype(BF16).reshape(2, 4, 2 * RA, HD)

    ab, sum_z = barrier((ab, sum_z))
    arrived = barrier(
        (swap(pick(ab, 1 - z // 4, 0), "z", 8, 4),)
        + tuple(shift(block_x(sum_z, k, 2 * HD), "x", 4, k) for k in (1, 2, 3))
    )
    ab = add_up([pick(ab, z // 4, 0), arrived[0]]).astype(BF16)
    s = add_up([block_x(sum_z, 0, 2 * HD), *arrived[1:]]).astype(BF16)
    arrived = barrier(
        tuple(swap(pick(ab, lax.rem(z, 4) ^ k, 0), "z", 8, k) for k in (1, 2, 3))
        + tuple(shift(block_y(s, k), Y, 4, k) for k in (1, 2, 3))
    )
    ab = add_up([pick(ab, lax.rem(z, 4), 0), *arrived[:3]])
    s = add_up([block_y(s, 0), *arrived[3:]])
    summed = jnp.concatenate([s, ab], axis=0)
    weight_grad = summed / F32(total_tokens)
    new_moment_one = 0.9 * moment_one + 0.1 * weight_grad
    new_moment_two = 0.999 * moment_two + 0.001 * weight_grad * weight_grad
    first_hat = new_moment_one / (1.0 - 0.9**STEP)
    second_hat = new_moment_two / (1.0 - 0.999**STEP)
    new_master = master - 0.001 * (first_hat / (jnp.sqrt(second_hat) + 1e-08) + 0.1 * master)
    return (
        query_grad,
        hidden_grad,
        new_master,
        new_moment_one,
        new_moment_two,
    )


def solution(mesh):
    names = ("x", "yh", "yl", "z", "c")
    fine = Mesh(mesh.devices.reshape(4, 2, 2, 8, 2), names)
    tokens = P(names, None)
    state = P(("yl", "z", "c"), ("x", "yh"))
    return jax.shard_map(
        body,
        mesh=fine,
        in_specs=(tokens,) * 6 + (P(("yl", "z", "c"), None), state, state, state),
        out_specs=(tokens, tokens, state, state, state),
        check_vma=False,
    )
```

```python
import jax
import jax.numpy as jnp
from jax import lax
from jax.experimental import pallas as pl
from jax.experimental.pallas import tpu as pltpu
from jax.sharding import Mesh, PartitionSpec as P

HD = 128
STEP = 10
ROPE_BASE = 1000000.0
GROUP = 5
KVH = 4
SCALE = HD**-0.5
RZ = 104
Y = ("yh", "yl")
F32 = jnp.float32
BF16 = jnp.bfloat16


def positions_in_row(segs):
    length = segs.shape[0]
    index = jnp.arange(length, dtype=jnp.int32)
    previous = jnp.concatenate([segs[:1] - 1, segs[:-1]])
    starts = jnp.where(segs != previous, index, jnp.zeros_like(index))
    return index - lax.cummax(starts)


def token_terms(segs, prompts, advs):
    pos = positions_in_row(segs)
    onehot = segs[:, None] == jnp.arange(prompts.shape[0], dtype=jnp.int32)[None, :]
    prompt_tok = jnp.sum(
        jnp.where(onehot, prompts[None, :], jnp.zeros_like(prompts)[None, :]), axis=1
    )
    adv_tok = jnp.sum(jnp.where(onehot, advs[None, :], jnp.zeros_like(advs)[None, :]), axis=1)
    return (pos, pos >= prompt_tok, adv_tok)


def shift(v, axis, n, k):
    return lax.ppermute(v, axis, [(i, (i + k) % n) for i in range(n)])


def swap(v, axis, n, bit):
    return lax.ppermute(v, axis, [(i, i ^ bit) for i in range(n)])


def total_of(v):
    for axis, n, bit in (
        ("c", 2, 1), ("x", 4, 1), ("x", 4, 2), ("yl", 2, 1), ("yh", 2, 1),
        ("z", 8, 1), ("z", 8, 2), ("z", 8, 4),
    ):
        v = v + swap(v, axis, n, bit)
    return v


def dot_nt(a, b):
    return lax.dot_general(a, b, (((1,), (1,)), ((), ())), preferred_element_type=F32)


def dot_tn(a, b):
    return lax.dot_general(a, b, (((0,), (0,)), ((), ())), preferred_element_type=F32)


def attention_kernel(kpre, vpre, q, up, cos, sin, start, weight, qg, kvg):
    length = kpre.shape[0]
    cosine, sine = cos[...], sin[...]
    kp = kpre[...]
    k = (kp * cosine + pltpu.roll(kp, HD // 2, 1) * sine).astype(BF16)
    v = vpre[...].astype(BF16)
    key_index = lax.broadcasted_iota(jnp.int32, (length, length), 0)
    query_index = lax.broadcasted_iota(jnp.int32, (length, length), 1)
    allowed = (key_index >= start[...]) & (key_index <= query_index)
    w = weight[...]
    dk = jnp.zeros((length, HD), F32)
    dv = jnp.zeros((length, HD), F32)
    for g in range(GROUP):
        cols = slice(g * HD, (g + 1) * HD)
        qh = q[:, cols]
        do = (up[:, cols].astype(F32) * w).astype(BF16)
        s = jnp.where(allowed, dot_nt(k, qh) * SCALE, F32(-1e30))
        e = jnp.exp(s - jnp.max(s, axis=0, keepdims=True))
        p = e * (1.0 / jnp.sum(e, axis=0, keepdims=True))
        low = p.astype(BF16)
        dp = dot_nt(v, do)
        delta = jnp.sum(low.astype(F32) * dp, axis=0, keepdims=True)
        ds = (p * (dp - delta)).astype(BF16)
        qg[:, cols] = (dot_tn(ds, k) * SCALE).astype(BF16)
        dk = dk + jnp.dot(ds, qh, preferred_element_type=F32)
        dv = dv + jnp.dot(low, do, preferred_element_type=F32)
    dk = dk * SCALE
    at = pl.multiple_of(pl.program_id(0) * HD, HD)
    kvg[:, pl.ds(at, HD)] = (dk * cosine - pltpu.roll(dk, HD // 2, 1) * sine).astype(BF16)
    kvg[:, pl.ds(at + KVH * HD, HD)] = dv.astype(BF16)


def attention_backward(kv_pre, queries, upstream, pos, weight):
    length = pos.shape[0]
    freq = ROPE_BASE ** (-(jnp.arange(HD // 2, dtype=F32) * 2.0 / HD))
    angle = pos.astype(F32)[:, None] * freq[None, :]
    cosine = jnp.concatenate([jnp.cos(angle), jnp.cos(angle)], axis=1)
    sine = jnp.concatenate([-jnp.sin(angle), jnp.sin(angle)], axis=1)
    start = (jnp.arange(length, dtype=jnp.int32) - pos)[None, :]
    whole = lambda shape: pl.BlockSpec(shape, lambda h: (0, 0))
    return pl.pallas_call(
        attention_kernel,
        grid=(KVH,),
        in_specs=[
            pl.BlockSpec((length, HD), lambda h: (0, h)),
            pl.BlockSpec((length, HD), lambda h: (0, h + KVH)),
            pl.BlockSpec((length, GROUP * HD), lambda h: (0, h)),
            pl.BlockSpec((length, GROUP * HD), lambda h: (0, h)),
            whole((length, HD)),
            whole((length, HD)),
            whole((1, length)),
            whole((length, 1)),
        ],
        out_specs=[
            pl.BlockSpec((length, GROUP * HD), lambda h: (0, h)),
            whole((length, 2 * KVH * HD)),
        ],
        out_shape=[
            jax.ShapeDtypeStruct((length, KVH * GROUP * HD), BF16),
            jax.ShapeDtypeStruct((length, 2 * KVH * HD), BF16),
        ],
        compiler_params=pltpu.CompilerParams(vmem_limit_bytes=32 * 2**20),
    )(kv_pre, kv_pre, queries, upstream, cosine, sine, start, weight[:, None])


def hidden_grad_kernel(kv, w, out):
    out[...] = dot_nt(kv[...], w[...]).astype(BF16)


def hidden_gradient(kv_grad, full_weight):
    length, cols = kv_grad.shape
    width = full_weight.shape[0]
    block = width // 8
    return pl.pallas_call(
        hidden_grad_kernel,
        grid=(8,),
        in_specs=[
            pl.BlockSpec((length, cols), lambda i: (0, 0)),
            pl.BlockSpec((block, cols), lambda i: (i, 0)),
        ],
        out_specs=pl.BlockSpec((length, block), lambda i: (0, i)),
        out_shape=jax.ShapeDtypeStruct((length, width), BF16),
        compiler_params=pltpu.CompilerParams(vmem_limit_bytes=48 * 2**20),
    )(kv_grad, full_weight)


def terms_kernel(place, ha, pair, *outs):
    for k in range(4):
        at = pl.multiple_of(lax.rem(place[0] + k, 4) * 2 * HD, 2 * HD)
        cols = pair[:, pl.ds(at, 2 * HD)]
        outs[k][...] = jnp.dot(ha[...], cols, preferred_element_type=F32).astype(BF16)


VMEM = pl.BlockSpec(memory_space=pltpu.VMEM)
SMEM = pl.BlockSpec(memory_space=pltpu.SMEM)


def terms(place, ha, pair):
    return pl.pallas_call(
        terms_kernel,
        in_specs=[SMEM, VMEM, VMEM],
        out_specs=[VMEM] * 4,
        out_shape=[jax.ShapeDtypeStruct((ha.shape[0], 2 * HD), BF16)] * 4,
        compiler_params=pltpu.CompilerParams(vmem_limit_bytes=24 * 2**20),
    )(place, ha, pair)


def turn_kernel(place, *refs):
    parts, outs, total = refs[:4], refs[4:8], refs[8]
    total[...] = add_up([r[...] for r in parts]).astype(BF16)
    half = total.shape[0] // 2
    for k in range(4):
        there = lax.rem(place[1] + k, 4)
        row = pl.multiple_of(lax.rem(there, 2) * half, half)
        col = pl.multiple_of(lax.div(there, 2) * HD, HD)
        outs[k][...] = total[pl.ds(row, half), pl.ds(col, HD)]


def turn(place, parts):
    rows = parts[0].shape[0]
    return pl.pallas_call(
        turn_kernel,
        in_specs=[SMEM] + [VMEM] * 4,
        out_specs=[VMEM] * 4,
        out_shape=[jax.ShapeDtypeStruct((rows // 2, HD), BF16)] * 4,
        scratch_shapes=[pltpu.VMEM(parts[0].shape, BF16)],
        compiler_params=pltpu.CompilerParams(vmem_limit_bytes=24 * 2**20),
    )(place, *parts)


def pick(v, index, axis):
    return lax.dynamic_index_in_dim(v, index, axis, keepdims=False)


def add_up(parts):
    total = parts[0].astype(F32)
    for part in parts[1:]:
        total = total + part.astype(F32)
    return total


def body(
    hidden,
    queries,
    upstream,
    segment_ids,
    prompt_lengths,
    advantages,
    kv_weight,
    master,
    moment_one,
    moment_two,
):
    barrier = lax.optimization_barrier
    x, z, c = lax.axis_index("x"), lax.axis_index("z"), lax.axis_index("c")
    y = lax.axis_index(Y)
    length, width = hidden.shape
    rows = kv_weight.shape[0]
    cols = kv_weight.shape[1]
    segs = segment_ids[0]
    full_weight = lax.all_gather(kv_weight, ("yl", "z", "c"), axis=0, tiled=True)
    pos, live, adv_tok = token_terms(segs, prompt_lengths[0], advantages[0])
    local_count = jnp.sum(live.astype(F32))
    count = total_of(jnp.broadcast_to(local_count, (8, 128)))[0, 0]
    total_tokens = length * 256
    factor = F32(total_tokens) / jnp.maximum(count, F32(1.0))
    weight = jnp.where(live, adv_tok * factor, jnp.zeros_like(adv_tok))

    hidden_t = hidden.T.reshape(16, 2, rows, length)
    mine = pick(hidden_t, c, 1)
    theirs = shift(pick(hidden_t, 1 - c, 1), "c", 2, 1)
    hidden_pair = jnp.concatenate([mine, theirs], axis=-1).reshape(2, 8, rows, 2 * length)
    hz = jnp.transpose(hidden_pair[:, :, :RZ], (1, 0, 2, 3)).reshape(16 * RZ, 2 * length)
    ha = hidden_pair[:, :, RZ:].reshape(16 * (rows - RZ), 2 * length)
    hidden, hz, ha = barrier((hidden, hz, ha))

    kv_pre = jnp.dot(hidden, full_weight, preferred_element_type=F32)
    query_grad, kv_grad = attention_backward(kv_pre, queries, upstream, pos, weight)
    pair = jnp.concatenate([kv_grad, shift(kv_grad, "c", 2, 1)], axis=0)

    part_z = jnp.dot(hz, pair, preferred_element_type=F32).astype(BF16)
    sum_z = lax.psum_scatter(part_z, "z", scatter_dimension=0, tiled=True)

    place = jnp.stack([x, y])

    out = barrier(tuple(terms(place, ha, pair)) + (kv_grad,))
    sent = tuple(shift(out[k], "x", 4, k) for k in (1, 2, 3))
    hidden_grad = hidden_gradient(out[4], full_weight)
    arrived = barrier(sent + (hidden_grad,))
    hidden_grad = arrived[3]
    out = turn(place, (out[0], *arrived[:3]))
    arrived = barrier(tuple(shift(out[k], Y, 4, k) for k in (1, 2, 3)))
    a = add_up([out[0], *arrived]).astype(BF16).reshape(2, 4, rows - RZ, HD)
    a = add_up([pick(a, z // 4, 0), swap(pick(a, 1 - z // 4, 0), "z", 8, 4)]).astype(BF16)
    sent = tuple(swap(pick(a, lax.rem(z, 4) ^ k, 0), "z", 8, k) for k in (1, 2, 3))

    blocks = jnp.stack([sum_z[:, j * HD : (j + 1) * HD] for j in range(8)]).reshape(16, RZ, HD)
    blocks, a = barrier((blocks, a))
    arrived = lax.all_to_all(blocks, ("x", *Y), 0, 0, tiled=True)
    arrived = barrier((arrived, *sent))
    summed = jnp.concatenate(
        [
            jnp.sum(arrived[0].astype(F32), axis=0),
            add_up([pick(a, lax.rem(z, 4), 0), *arrived[1:]]),
        ],
        axis=0,
    )
    weight_grad = summed / F32(total_tokens)
    new_moment_one = 0.9 * moment_one + 0.1 * weight_grad
    new_moment_two = 0.999 * moment_two + 0.001 * weight_grad * weight_grad
    first_hat = new_moment_one / (1.0 - 0.9**STEP)
    second_hat = new_moment_two / (1.0 - 0.999**STEP)
    new_master = master - 0.001 * (first_hat / (jnp.sqrt(second_hat) + 1e-08) + 0.1 * master)
    return (
        query_grad,
        hidden_grad,
        new_master,
        new_moment_one,
        new_moment_two,
    )


def solution(mesh):
    names = ("x", "yh", "yl", "z", "c")
    fine = Mesh(mesh.devices.reshape(4, 2, 2, 8, 2), names)
    tokens = P(names, None)
    state = P(("yl", "z", "c"), ("x", "yh"))
    return jax.shard_map(
        body,
        mesh=fine,
        in_specs=(tokens,) * 6 + (P(("yl", "z", "c"), None), state, state, state),
        out_specs=(tokens, tokens, state, state, state),
        check_vma=False,
    )
```

```python
import jax
import jax.numpy as jnp
from jax import lax
from jax.experimental import pallas as pl
from jax.experimental.pallas import tpu as pltpu
from jax.sharding import Mesh, PartitionSpec as P

HD = 128
STEP = 10
ROPE_BASE = 1000000.0
GROUP = 5
KVH = 4
SCALE = HD**-0.5
RZ = 96
Y = ("yh", "yl")
F32 = jnp.float32
BF16 = jnp.bfloat16


def positions_in_row(segs):
    length = segs.shape[0]
    index = jnp.arange(length, dtype=jnp.int32)
    previous = jnp.concatenate([segs[:1] - 1, segs[:-1]])
    starts = jnp.where(segs != previous, index, jnp.zeros_like(index))
    return index - lax.cummax(starts)


def token_terms(segs, prompts, advs):
    pos = positions_in_row(segs)
    onehot = segs[:, None] == jnp.arange(prompts.shape[0], dtype=jnp.int32)[None, :]
    prompt_tok = jnp.sum(
        jnp.where(onehot, prompts[None, :], jnp.zeros_like(prompts)[None, :]), axis=1
    )
    adv_tok = jnp.sum(jnp.where(onehot, advs[None, :], jnp.zeros_like(advs)[None, :]), axis=1)
    return (pos, pos >= prompt_tok, adv_tok)


def shift(v, axis, n, k):
    return lax.ppermute(v, axis, [(i, (i + k) % n) for i in range(n)])


def swap(v, axis, n, bit):
    return lax.ppermute(v, axis, [(i, i ^ bit) for i in range(n)])


def total_of(v):
    for axis, n, bit in (
        ("c", 2, 1), ("x", 4, 1), ("x", 4, 2), ("yl", 2, 1), ("yh", 2, 1),
        ("z", 8, 1), ("z", 8, 2), ("z", 8, 4),
    ):
        v = v + swap(v, axis, n, bit)
    return v


def dot_nt(a, b):
    return lax.dot_general(a, b, (((1,), (1,)), ((), ())), preferred_element_type=F32)


def dot_tn(a, b):
    return lax.dot_general(a, b, (((0,), (0,)), ((), ())), preferred_element_type=F32)


def attention_kernel(kpre, vpre, q, up, cos, sin, start, weight, qg, kvg):
    length = kpre.shape[0]
    cosine, sine = cos[...], sin[...]
    kp = kpre[...]
    k = (kp * cosine + pltpu.roll(kp, HD // 2, 1) * sine).astype(BF16)
    v = vpre[...].astype(BF16)
    key_index = lax.broadcasted_iota(jnp.int32, (length, length), 0)
    query_index = lax.broadcasted_iota(jnp.int32, (length, length), 1)
    allowed = (key_index >= start[...]) & (key_index <= query_index)
    w = weight[...]
    dk = jnp.zeros((length, HD), F32)
    dv = jnp.zeros((length, HD), F32)
    for g in range(GROUP):
        cols = slice(g * HD, (g + 1) * HD)
        qh = q[:, cols]
        do = (up[:, cols].astype(F32) * w).astype(BF16)
        s = jnp.where(allowed, dot_nt(k, qh) * SCALE, F32(-1e30))
        e = jnp.exp(s - jnp.max(s, axis=0, keepdims=True))
        p = e * (1.0 / jnp.sum(e, axis=0, keepdims=True))
        low = p.astype(BF16)
        dp = dot_nt(v, do)
        delta = jnp.sum(low.astype(F32) * dp, axis=0, keepdims=True)
        ds = (p * (dp - delta)).astype(BF16)
        qg[:, cols] = (dot_tn(ds, k) * SCALE).astype(BF16)
        dk = dk + jnp.dot(ds, qh, preferred_element_type=F32)
        dv = dv + jnp.dot(low, do, preferred_element_type=F32)
    dk = dk * SCALE
    at = pl.multiple_of(pl.program_id(0) * HD, HD)
    kvg[:, pl.ds(at, HD)] = (dk * cosine - pltpu.roll(dk, HD // 2, 1) * sine).astype(BF16)
    kvg[:, pl.ds(at + KVH * HD, HD)] = dv.astype(BF16)


def attention_backward(kv_pre, queries, upstream, pos, weight):
    length = pos.shape[0]
    freq = ROPE_BASE ** (-(jnp.arange(HD // 2, dtype=F32) * 2.0 / HD))
    angle = pos.astype(F32)[:, None] * freq[None, :]
    cosine = jnp.concatenate([jnp.cos(angle), jnp.cos(angle)], axis=1)
    sine = jnp.concatenate([-jnp.sin(angle), jnp.sin(angle)], axis=1)
    start = (jnp.arange(length, dtype=jnp.int32) - pos)[None, :]
    whole = lambda shape: pl.BlockSpec(shape, lambda h: (0, 0))
    return pl.pallas_call(
        attention_kernel,
        grid=(KVH,),
        in_specs=[
            pl.BlockSpec((length, HD), lambda h: (0, h)),
            pl.BlockSpec((length, HD), lambda h: (0, h + KVH)),
            pl.BlockSpec((length, GROUP * HD), lambda h: (0, h)),
            pl.BlockSpec((length, GROUP * HD), lambda h: (0, h)),
            whole((length, HD)),
            whole((length, HD)),
            whole((1, length)),
            whole((length, 1)),
        ],
        out_specs=[
            pl.BlockSpec((length, GROUP * HD), lambda h: (0, h)),
            whole((length, 2 * KVH * HD)),
        ],
        out_shape=[
            jax.ShapeDtypeStruct((length, KVH * GROUP * HD), BF16),
            jax.ShapeDtypeStruct((length, 2 * KVH * HD), BF16),
        ],
        compiler_params=pltpu.CompilerParams(vmem_limit_bytes=32 * 2**20),
    )(kv_pre, kv_pre, queries, upstream, cosine, sine, start, weight[:, None])


def hidden_grad_kernel(kv, w, out):
    out[...] = dot_nt(kv[...], w[...]).astype(BF16)


def hidden_gradient(kv_grad, full_weight):
    length, cols = kv_grad.shape
    width = full_weight.shape[0]
    block = width // 8
    return pl.pallas_call(
        hidden_grad_kernel,
        grid=(8,),
        in_specs=[
            pl.BlockSpec((length, cols), lambda i: (0, 0)),
            pl.BlockSpec((block, cols), lambda i: (i, 0)),
        ],
        out_specs=pl.BlockSpec((length, block), lambda i: (0, i)),
        out_shape=jax.ShapeDtypeStruct((length, width), BF16),
        compiler_params=pltpu.CompilerParams(vmem_limit_bytes=48 * 2**20),
    )(kv_grad, full_weight)


def first_terms_kernel(h, pair, out):
    term = jnp.dot(h[0], pair[...], preferred_element_type=F32).astype(BF16)
    rows = h.shape[1]
    for j in range(8):
        out[j * rows : (j + 1) * rows, :] = term[:, j * HD : (j + 1) * HD]


def first_terms(hz, pair):
    planes, rows, depth = hz.shape
    return pl.pallas_call(
        first_terms_kernel,
        grid=(planes,),
        in_specs=[
            pl.BlockSpec((1, rows, depth), lambda i: (i, 0, 0)),
            pl.BlockSpec(pair.shape, lambda i: (0, 0)),
        ],
        out_specs=pl.BlockSpec((8 * rows, HD), lambda i: (i, 0)),
        out_shape=jax.ShapeDtypeStruct((planes * 8 * rows, HD), BF16),
        compiler_params=pltpu.CompilerParams(vmem_limit_bytes=24 * 2**20),
    )(hz, pair)


def terms_kernel(place, ha, pair, *outs):
    for k in range(4):
        at = pl.multiple_of(lax.rem(place[0] + k, 4) * 2 * HD, 2 * HD)
        cols = pair[:, pl.ds(at, 2 * HD)]
        outs[k][...] = jnp.dot(ha[...], cols, preferred_element_type=F32).astype(BF16)


VMEM = pl.BlockSpec(memory_space=pltpu.VMEM)
SMEM = pl.BlockSpec(memory_space=pltpu.SMEM)


def terms(place, ha, pair):
    return pl.pallas_call(
        terms_kernel,
        in_specs=[SMEM, VMEM, VMEM],
        out_specs=[VMEM] * 4,
        out_shape=[jax.ShapeDtypeStruct((ha.shape[0], 2 * HD), BF16)] * 4,
        compiler_params=pltpu.CompilerParams(vmem_limit_bytes=24 * 2**20),
    )(place, ha, pair)


def turn_kernel(place, *refs):
    parts, outs, total = refs[:4], refs[4:8], refs[8]
    total[...] = add_up([r[...] for r in parts]).astype(BF16)
    half = total.shape[0] // 2
    for k in range(4):
        there = lax.rem(place[1] + k, 4)
        row = pl.multiple_of(lax.rem(there, 2) * half, half)
        col = pl.multiple_of(lax.div(there, 2) * HD, HD)
        outs[k][...] = total[pl.ds(row, half), pl.ds(col, HD)]


def turn(place, parts):
    rows = parts[0].shape[0]
    return pl.pallas_call(
        turn_kernel,
        in_specs=[SMEM] + [VMEM] * 4,
        out_specs=[VMEM] * 4,
        out_shape=[jax.ShapeDtypeStruct((rows // 2, HD), BF16)] * 4,
        scratch_shapes=[pltpu.VMEM(parts[0].shape, BF16)],
        compiler_params=pltpu.CompilerParams(vmem_limit_bytes=24 * 2**20),
    )(place, *parts)


def pick(v, index, axis):
    return lax.dynamic_index_in_dim(v, index, axis, keepdims=False)


def add_up(parts):
    total = parts[0].astype(F32)
    for part in parts[1:]:
        total = total + part.astype(F32)
    return total


def body(
    hidden,
    queries,
    upstream,
    segment_ids,
    prompt_lengths,
    advantages,
    kv_weight,
    master,
    moment_one,
    moment_two,
):
    barrier = lax.optimization_barrier
    x, z, c = lax.axis_index("x"), lax.axis_index("z"), lax.axis_index("c")
    y = lax.axis_index(Y)
    length, width = hidden.shape
    rows = kv_weight.shape[0]
    cols = kv_weight.shape[1]
    segs = segment_ids[0]
    full_weight = lax.all_gather(kv_weight, ("yl", "z", "c"), axis=0, tiled=True)
    pos, live, adv_tok = token_terms(segs, prompt_lengths[0], advantages[0])
    local_count = jnp.sum(live.astype(F32))
    count = total_of(jnp.broadcast_to(local_count, (8, 128)))[0, 0]
    total_tokens = length * 256
    factor = F32(total_tokens) / jnp.maximum(count, F32(1.0))
    weight = jnp.where(live, adv_tok * factor, jnp.zeros_like(adv_tok))

    hidden_t = hidden.T.reshape(16, 2, rows, length)
    mine = pick(hidden_t, c, 1)
    theirs = shift(pick(hidden_t, 1 - c, 1), "c", 2, 1)
    hidden_pair = jnp.concatenate([mine, theirs], axis=-1).reshape(2, 8, rows, 2 * length)
    hz = jnp.transpose(hidden_pair[:, :, :RZ], (1, 0, 2, 3)).reshape(8, 2 * RZ, 2 * length)
    ha = hidden_pair[:, :, RZ:].reshape(16 * (rows - RZ), 2 * length)
    hidden, hz, ha = barrier((hidden, hz, ha))

    kv_pre = jnp.dot(hidden, full_weight, preferred_element_type=F32)
    query_grad, kv_grad = attention_backward(kv_pre, queries, upstream, pos, weight)
    pair = jnp.concatenate([kv_grad, shift(kv_grad, "c", 2, 1)], axis=0)

    sum_z = lax.psum_scatter(first_terms(hz, pair), "z", scatter_dimension=0, tiled=True)

    place = jnp.stack([x, y])

    out = barrier(tuple(terms(place, ha, pair)) + (kv_grad,))
    sent = tuple(shift(out[k], "x", 4, k) for k in (1, 2, 3))
    hidden_grad = hidden_gradient(out[4], full_weight)
    arrived = barrier(sent + (hidden_grad,))
    hidden_grad = arrived[3]
    out = turn(place, (out[0], *arrived[:3]))
    arrived = barrier(tuple(shift(out[k], Y, 4, k) for k in (1, 2, 3)))
    a = add_up([out[0], *arrived]).astype(BF16).reshape(2, 4, rows - RZ, HD)
    a = add_up([pick(a, z // 4, 0), swap(pick(a, 1 - z // 4, 0), "z", 8, 4)]).astype(BF16)
    sent = tuple(swap(pick(a, lax.rem(z, 4) ^ k, 0), "z", 8, k) for k in (1, 2, 3))

    blocks = sum_z.reshape(16, RZ, HD)
    blocks, a = barrier((blocks, a))
    arrived = lax.all_to_all(blocks, ("x", *Y), 0, 0, tiled=True)
    arrived = barrier((arrived, *sent))
    summed = jnp.concatenate(
        [
            jnp.sum(arrived[0].astype(F32), axis=0),
            add_up([pick(a, lax.rem(z, 4), 0), *arrived[1:]]),
        ],
        axis=0,
    )
    weight_grad = summed / F32(total_tokens)
    new_moment_one = 0.9 * moment_one + 0.1 * weight_grad
    new_moment_two = 0.999 * moment_two + 0.001 * weight_grad * weight_grad
    first_hat = new_moment_one / (1.0 - 0.9**STEP)
    second_hat = new_moment_two / (1.0 - 0.999**STEP)
    new_master = master - 0.001 * (first_hat / (jnp.sqrt(second_hat) + 1e-08) + 0.1 * master)
    return (
        query_grad,
        hidden_grad,
        new_master,
        new_moment_one,
        new_moment_two,
    )


def solution(mesh):
    names = ("x", "yh", "yl", "z", "c")
    fine = Mesh(mesh.devices.reshape(4, 2, 2, 8, 2), names)
    tokens = P(names, None)
    state = P(("yl", "z", "c"), ("x", "yh"))
    return jax.shard_map(
        body,
        mesh=fine,
        in_specs=(tokens,) * 6 + (P(("yl", "z", "c"), None), state, state, state),
        out_specs=(tokens, tokens, state, state, state),
        check_vma=False,
    )
```

```python
import jax
import jax.numpy as jnp
from jax import lax
from jax.experimental import pallas as pl
from jax.experimental.pallas import tpu as pltpu
from jax.sharding import Mesh, PartitionSpec as P

HD = 128
STEP = 10
ROPE_BASE = 1000000.0
GROUP = 5
KVH = 4
SCALE = HD**-0.5
RZ = 96
Y = ("yh", "yl")
F32 = jnp.float32
BF16 = jnp.bfloat16


def positions_in_row(segs):
    length = segs.shape[0]
    index = jnp.arange(length, dtype=jnp.int32)
    previous = jnp.concatenate([segs[:1] - 1, segs[:-1]])
    starts = jnp.where(segs != previous, index, jnp.zeros_like(index))
    return index - lax.cummax(starts)


def token_terms(segs, prompts, advs):
    pos = positions_in_row(segs)
    onehot = segs[:, None] == jnp.arange(prompts.shape[0], dtype=jnp.int32)[None, :]
    prompt_tok = jnp.sum(
        jnp.where(onehot, prompts[None, :], jnp.zeros_like(prompts)[None, :]), axis=1
    )
    adv_tok = jnp.sum(jnp.where(onehot, advs[None, :], jnp.zeros_like(advs)[None, :]), axis=1)
    return (pos, pos >= prompt_tok, adv_tok)


def shift(v, axis, n, k):
    return lax.ppermute(v, axis, [(i, (i + k) % n) for i in range(n)])


def swap(v, axis, n, bit):
    return lax.ppermute(v, axis, [(i, i ^ bit) for i in range(n)])


def total_of(v):
    for axis, n, bit in (
        ("c", 2, 1), ("x", 4, 1), ("x", 4, 2), ("yl", 2, 1), ("yh", 2, 1),
        ("z", 8, 1), ("z", 8, 2), ("z", 8, 4),
    ):
        v = v + swap(v, axis, n, bit)
    return v


def dot_nt(a, b):
    return lax.dot_general(a, b, (((1,), (1,)), ((), ())), preferred_element_type=F32)


def dot_tn(a, b):
    return lax.dot_general(a, b, (((0,), (0,)), ((), ())), preferred_element_type=F32)


def attention_kernel(kpre, vpre, q, up, cos, sin, start, weight, qg, kvg):
    length = kpre.shape[0]
    cosine, sine = cos[...], sin[...]
    kp = kpre[...]
    k = (kp * cosine + pltpu.roll(kp, HD // 2, 1) * sine).astype(BF16)
    v = vpre[...].astype(BF16)
    key_index = lax.broadcasted_iota(jnp.int32, (length, length), 0)
    query_index = lax.broadcasted_iota(jnp.int32, (length, length), 1)
    allowed = (key_index >= start[...]) & (key_index <= query_index)
    w = weight[...]
    dk = jnp.zeros((length, HD), F32)
    dv = jnp.zeros((length, HD), F32)
    for g in range(GROUP):
        cols = slice(g * HD, (g + 1) * HD)
        qh = q[:, cols]
        do = (up[:, cols].astype(F32) * w).astype(BF16)
        s = jnp.where(allowed, dot_nt(k, qh) * SCALE, F32(-1e30))
        e = jnp.exp(s - jnp.max(s, axis=0, keepdims=True))
        p = e * (1.0 / jnp.sum(e, axis=0, keepdims=True))
        low = p.astype(BF16)
        dp = dot_nt(v, do)
        delta = jnp.sum(low.astype(F32) * dp, axis=0, keepdims=True)
        ds = (p * (dp - delta)).astype(BF16)
        qg[:, cols] = (dot_tn(ds, k) * SCALE).astype(BF16)
        dk = dk + jnp.dot(ds, qh, preferred_element_type=F32)
        dv = dv + jnp.dot(low, do, preferred_element_type=F32)
    dk = dk * SCALE
    at = pl.multiple_of(pl.program_id(0) * HD, HD)
    kvg[:, pl.ds(at, HD)] = (dk * cosine - pltpu.roll(dk, HD // 2, 1) * sine).astype(BF16)
    kvg[:, pl.ds(at + KVH * HD, HD)] = dv.astype(BF16)


def attention_backward(kv_pre, queries, upstream, pos, weight):
    length = pos.shape[0]
    freq = ROPE_BASE ** (-(jnp.arange(HD // 2, dtype=F32) * 2.0 / HD))
    angle = pos.astype(F32)[:, None] * freq[None, :]
    cosine = jnp.concatenate([jnp.cos(angle), jnp.cos(angle)], axis=1)
    sine = jnp.concatenate([-jnp.sin(angle), jnp.sin(angle)], axis=1)
    start = (jnp.arange(length, dtype=jnp.int32) - pos)[None, :]
    whole = lambda shape: pl.BlockSpec(shape, lambda h: (0, 0))
    return pl.pallas_call(
        attention_kernel,
        grid=(KVH,),
        in_specs=[
            pl.BlockSpec((length, HD), lambda h: (0, h)),
            pl.BlockSpec((length, HD), lambda h: (0, h + KVH)),
            pl.BlockSpec((length, GROUP * HD), lambda h: (0, h)),
            pl.BlockSpec((length, GROUP * HD), lambda h: (0, h)),
            whole((length, HD)),
            whole((length, HD)),
            whole((1, length)),
            whole((length, 1)),
        ],
        out_specs=[
            pl.BlockSpec((length, GROUP * HD), lambda h: (0, h)),
            whole((length, 2 * KVH * HD)),
        ],
        out_shape=[
            jax.ShapeDtypeStruct((length, KVH * GROUP * HD), BF16),
            jax.ShapeDtypeStruct((length, 2 * KVH * HD), BF16),
        ],
        compiler_params=pltpu.CompilerParams(vmem_limit_bytes=32 * 2**20),
    )(kv_pre, kv_pre, queries, upstream, cosine, sine, start, weight[:, None])


def hidden_grad_kernel(kv, w, out):
    out[...] = dot_nt(kv[...], w[...]).astype(BF16)


def hidden_gradient(kv_grad, full_weight):
    length, cols = kv_grad.shape
    width = full_weight.shape[0]
    block = width // 8
    return pl.pallas_call(
        hidden_grad_kernel,
        grid=(8,),
        in_specs=[
            pl.BlockSpec((length, cols), lambda i: (0, 0)),
            pl.BlockSpec((block, cols), lambda i: (i, 0)),
        ],
        out_specs=pl.BlockSpec((length, block), lambda i: (0, i)),
        out_shape=jax.ShapeDtypeStruct((length, width), BF16),
        compiler_params=pltpu.CompilerParams(vmem_limit_bytes=48 * 2**20),
    )(kv_grad, full_weight)


def first_terms_kernel(h, pair, out):
    planes, rows, depth = h.shape
    block = h[...].reshape(planes * rows, depth)
    term = jnp.dot(block, pair[...], preferred_element_type=F32).astype(BF16)
    for p in range(planes):
        for j in range(8):
            at = (8 * p + j) * rows
            out[at : at + rows, :] = term[p * rows : (p + 1) * rows, j * HD : (j + 1) * HD]


def first_terms(hz, pair):
    planes, rows, depth = hz.shape
    return pl.pallas_call(
        first_terms_kernel,
        grid=(planes // 2,),
        in_specs=[
            pl.BlockSpec((2, rows, depth), lambda i: (i, 0, 0)),
            pl.BlockSpec(pair.shape, lambda i: (0, 0)),
        ],
        out_specs=pl.BlockSpec((16 * rows, HD), lambda i: (i, 0)),
        out_shape=jax.ShapeDtypeStruct((planes * 8 * rows, HD), BF16),
        compiler_params=pltpu.CompilerParams(vmem_limit_bytes=24 * 2**20),
    )(hz, pair)


def terms_kernel(place, ha, pair, *outs):
    for k in range(4):
        at = pl.multiple_of(lax.rem(place[0] + k, 4) * 2 * HD, 2 * HD)
        cols = pair[:, pl.ds(at, 2 * HD)]
        outs[k][...] = jnp.dot(ha[...], cols, preferred_element_type=F32).astype(BF16)


VMEM = pl.BlockSpec(memory_space=pltpu.VMEM)
SMEM = pl.BlockSpec(memory_space=pltpu.SMEM)


def terms(place, ha, pair):
    return pl.pallas_call(
        terms_kernel,
        in_specs=[SMEM, VMEM, VMEM],
        out_specs=[VMEM] * 4,
        out_shape=[jax.ShapeDtypeStruct((ha.shape[0], 2 * HD), BF16)] * 4,
        compiler_params=pltpu.CompilerParams(vmem_limit_bytes=24 * 2**20),
    )(place, ha, pair)


def turn_kernel(place, *refs):
    parts, outs, total = refs[:4], refs[4:8], refs[8]
    total[...] = add_up([r[...] for r in parts]).astype(BF16)
    half = total.shape[0] // 2
    for k in range(4):
        there = lax.rem(place[1] + k, 4)
        row = pl.multiple_of(lax.rem(there, 2) * half, half)
        col = pl.multiple_of(lax.div(there, 2) * HD, HD)
        outs[k][...] = total[pl.ds(row, half), pl.ds(col, HD)]


def turn(place, parts):
    rows = parts[0].shape[0]
    return pl.pallas_call(
        turn_kernel,
        in_specs=[SMEM] + [VMEM] * 4,
        out_specs=[VMEM] * 4,
        out_shape=[jax.ShapeDtypeStruct((rows // 2, HD), BF16)] * 4,
        scratch_shapes=[pltpu.VMEM(parts[0].shape, BF16)],
        compiler_params=pltpu.CompilerParams(vmem_limit_bytes=24 * 2**20),
    )(place, *parts)


def pick(v, index, axis):
    return lax.dynamic_index_in_dim(v, index, axis, keepdims=False)


def add_up(parts):
    total = parts[0].astype(F32)
    for part in parts[1:]:
        total = total + part.astype(F32)
    return total


def body(
    hidden,
    queries,
    upstream,
    segment_ids,
    prompt_lengths,
    advantages,
    kv_weight,
    master,
    moment_one,
    moment_two,
):
    barrier = lax.optimization_barrier
    x, z, c = lax.axis_index("x"), lax.axis_index("z"), lax.axis_index("c")
    y = lax.axis_index(Y)
    length, width = hidden.shape
    rows = kv_weight.shape[0]
    cols = kv_weight.shape[1]
    segs = segment_ids[0]
    full_weight = lax.all_gather(kv_weight, ("yl", "z", "c"), axis=0, tiled=True)
    pos, live, adv_tok = token_terms(segs, prompt_lengths[0], advantages[0])
    local_count = jnp.sum(live.astype(F32))
    count = total_of(jnp.broadcast_to(local_count, (8, 128)))[0, 0]
    total_tokens = length * 256
    factor = F32(total_tokens) / jnp.maximum(count, F32(1.0))
    weight = jnp.where(live, adv_tok * factor, jnp.zeros_like(adv_tok))

    hidden_t = hidden.T.reshape(16, 2, rows, length)
    mine = pick(hidden_t, c, 1)
    theirs = shift(pick(hidden_t, 1 - c, 1), "c", 2, 1)
    hidden_pair = jnp.concatenate([mine, theirs], axis=-1).reshape(2, 8, rows, 2 * length)
    hz = jnp.transpose(hidden_pair[:, :, :RZ], (1, 0, 2, 3)).reshape(8, 2 * RZ, 2 * length)
    ha = hidden_pair[:, :, RZ:].reshape(16 * (rows - RZ), 2 * length)
    hidden, hz, ha = barrier((hidden, hz, ha))

    kv_pre = jnp.dot(hidden, full_weight, preferred_element_type=F32)
    query_grad, kv_grad = attention_backward(kv_pre, queries, upstream, pos, weight)
    pair = jnp.concatenate([kv_grad, shift(kv_grad, "c", 2, 1)], axis=0)

    sum_z = lax.psum_scatter(first_terms(hz, pair), "z", scatter_dimension=0, tiled=True)

    place = jnp.stack([x, y])

    out = barrier(tuple(terms(place, ha, pair)) + (kv_grad,))
    sent = tuple(shift(out[k], "x", 4, k) for k in (1, 2, 3))
    hidden_grad = hidden_gradient(out[4], full_weight)
    arrived = barrier(sent + (hidden_grad,))
    hidden_grad = arrived[3]
    out = turn(place, (out[0], *arrived[:3]))
    arrived = barrier(tuple(shift(out[k], Y, 4, k) for k in (1, 2, 3)))
    a = add_up([out[0], *arrived]).astype(BF16).reshape(2, 4, rows - RZ, HD)
    blocks = lax.all_to_all(sum_z.reshape(16, RZ, HD), ("x", *Y), 0, 0, tiled=True)
    theirs = swap(pick(a, 1 - z // 4, 0), "z", 8, 4)
    theirs, a, _ = barrier((theirs, a, sum_z))
    a = add_up([pick(a, z // 4, 0), theirs]).astype(BF16)
    sent = tuple(swap(pick(a, lax.rem(z, 4) ^ k, 0), "z", 8, k) for k in (1, 2, 3))
    arrived = barrier((blocks, *sent))
    summed = jnp.concatenate(
        [
            jnp.sum(arrived[0].astype(F32), axis=0),
            add_up([pick(a, lax.rem(z, 4), 0), *arrived[1:]]),
        ],
        axis=0,
    )
    weight_grad = summed / F32(total_tokens)
    new_moment_one = 0.9 * moment_one + 0.1 * weight_grad
    new_moment_two = 0.999 * moment_two + 0.001 * weight_grad * weight_grad
    first_hat = new_moment_one / (1.0 - 0.9**STEP)
    second_hat = new_moment_two / (1.0 - 0.999**STEP)
    new_master = master - 0.001 * (first_hat / (jnp.sqrt(second_hat) + 1e-08) + 0.1 * master)
    return (
        query_grad,
        hidden_grad,
        new_master,
        new_moment_one,
        new_moment_two,
    )


def solution(mesh):
    names = ("x", "yh", "yl", "z", "c")
    fine = Mesh(mesh.devices.reshape(4, 2, 2, 8, 2), names)
    tokens = P(names, None)
    state = P(("yl", "z", "c"), ("x", "yh"))
    return jax.shard_map(
        body,
        mesh=fine,
        in_specs=(tokens,) * 6 + (P(("yl", "z", "c"), None), state, state, state),
        out_specs=(tokens, tokens, state, state, state),
        check_vma=False,
    )
```

```python
import jax
import jax.numpy as jnp
from jax import lax
from jax.experimental import pallas as pl
from jax.experimental.pallas import tpu as pltpu
from jax.sharding import Mesh, PartitionSpec as P

HD = 128
STEP = 10
ROPE_BASE = 1000000.0
GROUP = 5
KVH = 4
SCALE = HD**-0.5
RZ = 96
Y = ("yh", "yl")
F32 = jnp.float32
BF16 = jnp.bfloat16


def positions_in_row(segs):
    length = segs.shape[0]
    index = jnp.arange(length, dtype=jnp.int32)
    previous = jnp.concatenate([segs[:1] - 1, segs[:-1]])
    starts = jnp.where(segs != previous, index, jnp.zeros_like(index))
    return index - lax.cummax(starts)


def token_terms(segs, prompts, advs):
    pos = positions_in_row(segs)
    onehot = segs[:, None] == jnp.arange(prompts.shape[0], dtype=jnp.int32)[None, :]
    prompt_tok = jnp.sum(
        jnp.where(onehot, prompts[None, :], jnp.zeros_like(prompts)[None, :]), axis=1
    )
    adv_tok = jnp.sum(jnp.where(onehot, advs[None, :], jnp.zeros_like(advs)[None, :]), axis=1)
    return (pos, pos >= prompt_tok, adv_tok)


def shift(v, axis, n, k):
    return lax.ppermute(v, axis, [(i, (i + k) % n) for i in range(n)])


def swap(v, axis, n, bit):
    return lax.ppermute(v, axis, [(i, i ^ bit) for i in range(n)])


def total_of(v):
    for axis, n, bit in (
        ("c", 2, 1), ("x", 4, 1), ("x", 4, 2), ("yl", 2, 1), ("yh", 2, 1),
        ("z", 8, 1), ("z", 8, 2), ("z", 8, 4),
    ):
        v = v + swap(v, axis, n, bit)
    return v


def dot_nt(a, b):
    return lax.dot_general(a, b, (((1,), (1,)), ((), ())), preferred_element_type=F32)


def dot_tn(a, b):
    return lax.dot_general(a, b, (((0,), (0,)), ((), ())), preferred_element_type=F32)


def attention_kernel(kpre, vpre, q, up, cos, sin, start, weight, qg, kvg):
    length = kpre.shape[0]
    half = length // 2
    cosine, sine = cos[...], sin[...]
    kp = kpre[...]
    k = (kp * cosine + pltpu.roll(kp, HD // 2, 1) * sine).astype(BF16)
    v = vpre[...].astype(BF16)
    dk, dv = [], []
    for part in range(2):
        rows, keys = slice(part * half, (part + 1) * half), (part + 1) * half
        kh, vh = k[:keys], v[:keys]
        key_index = lax.broadcasted_iota(jnp.int32, (keys, half), 0)
        query_index = lax.broadcasted_iota(jnp.int32, (keys, half), 1) + part * half
        allowed = (key_index >= start[:, rows]) & (key_index <= query_index)
        allowed = jnp.concatenate([allowed.astype(F32)] * GROUP, axis=1) > 0
        w = weight[rows, :]
        cols = [slice(g * HD, (g + 1) * HD) for g in range(GROUP)]
        qh = jnp.concatenate([q[rows, c] for c in cols], axis=0)
        do = jnp.concatenate([(up[rows, c].astype(F32) * w).astype(BF16) for c in cols], axis=0)
        s = jnp.where(allowed, dot_nt(kh, qh) * SCALE, F32(-1e30))
        e = jnp.exp(s - jnp.max(s, axis=0, keepdims=True))
        p = e * (1.0 / jnp.sum(e, axis=0, keepdims=True))
        low = p.astype(BF16)
        dp = dot_nt(vh, do)
        delta = jnp.sum(low.astype(F32) * dp, axis=0, keepdims=True)
        ds = (p * (dp - delta)).astype(BF16)
        dq = (dot_tn(ds, kh) * SCALE).astype(BF16)
        for g in range(GROUP):
            qg[rows, cols[g]] = dq[g * half : (g + 1) * half]
        dk.append(jnp.dot(ds, qh, preferred_element_type=F32))
        dv.append(jnp.dot(low, do, preferred_element_type=F32))
    dk = jnp.concatenate([dk[0] + dk[1][:half], dk[1][half:]], axis=0) * SCALE
    dv = jnp.concatenate([dv[0] + dv[1][:half], dv[1][half:]], axis=0)
    at = pl.multiple_of(pl.program_id(0) * HD, HD)
    kvg[:, pl.ds(at, HD)] = (dk * cosine - pltpu.roll(dk, HD // 2, 1) * sine).astype(BF16)
    kvg[:, pl.ds(at + KVH * HD, HD)] = dv.astype(BF16)


def attention_backward(kv_pre, queries, upstream, pos, weight):
    length = pos.shape[0]
    freq = ROPE_BASE ** (-(jnp.arange(HD // 2, dtype=F32) * 2.0 / HD))
    angle = pos.astype(F32)[:, None] * freq[None, :]
    cosine = jnp.concatenate([jnp.cos(angle), jnp.cos(angle)], axis=1)
    sine = jnp.concatenate([-jnp.sin(angle), jnp.sin(angle)], axis=1)
    start = (jnp.arange(length, dtype=jnp.int32) - pos)[None, :]
    whole = lambda shape: pl.BlockSpec(shape, lambda h: (0, 0))
    return pl.pallas_call(
        attention_kernel,
        grid=(KVH,),
        in_specs=[
            pl.BlockSpec((length, HD), lambda h: (0, h)),
            pl.BlockSpec((length, HD), lambda h: (0, h + KVH)),
            pl.BlockSpec((length, GROUP * HD), lambda h: (0, h)),
            pl.BlockSpec((length, GROUP * HD), lambda h: (0, h)),
            whole((length, HD)),
            whole((length, HD)),
            whole((1, length)),
            whole((length, 1)),
        ],
        out_specs=[
            pl.BlockSpec((length, GROUP * HD), lambda h: (0, h)),
            whole((length, 2 * KVH * HD)),
        ],
        out_shape=[
            jax.ShapeDtypeStruct((length, KVH * GROUP * HD), BF16),
            jax.ShapeDtypeStruct((length, 2 * KVH * HD), BF16),
        ],
        compiler_params=pltpu.CompilerParams(vmem_limit_bytes=32 * 2**20),
    )(kv_pre, kv_pre, queries, upstream, cosine, sine, start, weight[:, None])


def hidden_grad_kernel(kv, w, out):
    out[...] = dot_nt(kv[...], w[...]).astype(BF16)


def hidden_gradient(kv_grad, full_weight):
    length, cols = kv_grad.shape
    width = full_weight.shape[0]
    block = width // 8
    return pl.pallas_call(
        hidden_grad_kernel,
        grid=(8,),
        in_specs=[
            pl.BlockSpec((length, cols), lambda i: (0, 0)),
            pl.BlockSpec((block, cols), lambda i: (i, 0)),
        ],
        out_specs=pl.BlockSpec((length, block), lambda i: (0, i)),
        out_shape=jax.ShapeDtypeStruct((length, width), BF16),
        compiler_params=pltpu.CompilerParams(vmem_limit_bytes=48 * 2**20),
    )(kv_grad, full_weight)


def first_terms_kernel(h, pair, out):
    planes, rows, depth = h.shape
    block = h[...].reshape(planes * rows, depth)
    term = jnp.dot(block, pair[...], preferred_element_type=F32).astype(BF16)
    for p in range(planes):
        for j in range(8):
            at = (8 * p + j) * rows
            out[at : at + rows, :] = term[p * rows : (p + 1) * rows, j * HD : (j + 1) * HD]


def first_terms(hz, pair):
    planes, rows, depth = hz.shape
    return pl.pallas_call(
        first_terms_kernel,
        grid=(planes // 2,),
        in_specs=[
            pl.BlockSpec((2, rows, depth), lambda i: (i, 0, 0)),
            pl.BlockSpec(pair.shape, lambda i: (0, 0)),
        ],
        out_specs=pl.BlockSpec((16 * rows, HD), lambda i: (i, 0)),
        out_shape=jax.ShapeDtypeStruct((planes * 8 * rows, HD), BF16),
        compiler_params=pltpu.CompilerParams(vmem_limit_bytes=24 * 2**20),
    )(hz, pair)


def terms_kernel(place, ha, pair, *outs):
    for k in range(4):
        at = pl.multiple_of(lax.rem(place[0] + k, 4) * 2 * HD, 2 * HD)
        cols = pair[:, pl.ds(at, 2 * HD)]
        outs[k][...] = jnp.dot(ha[...], cols, preferred_element_type=F32).astype(BF16)


VMEM = pl.BlockSpec(memory_space=pltpu.VMEM)
SMEM = pl.BlockSpec(memory_space=pltpu.SMEM)


def terms(place, ha, pair):
    return pl.pallas_call(
        terms_kernel,
        in_specs=[SMEM, VMEM, VMEM],
        out_specs=[VMEM] * 4,
        out_shape=[jax.ShapeDtypeStruct((ha.shape[0], 2 * HD), BF16)] * 4,
        compiler_params=pltpu.CompilerParams(vmem_limit_bytes=24 * 2**20),
    )(place, ha, pair)


def turn_kernel(place, *refs):
    parts, outs, total = refs[:4], refs[4:8], refs[8]
    total[...] = add_up([r[...] for r in parts]).astype(BF16)
    half = total.shape[0] // 2
    for k in range(4):
        there = lax.rem(place[1] + k, 4)
        row = pl.multiple_of(lax.rem(there, 2) * half, half)
        col = pl.multiple_of(lax.div(there, 2) * HD, HD)
        outs[k][...] = total[pl.ds(row, half), pl.ds(col, HD)]


def turn(place, parts):
    rows = parts[0].shape[0]
    return pl.pallas_call(
        turn_kernel,
        in_specs=[SMEM] + [VMEM] * 4,
        out_specs=[VMEM] * 4,
        out_shape=[jax.ShapeDtypeStruct((rows // 2, HD), BF16)] * 4,
        scratch_shapes=[pltpu.VMEM(parts[0].shape, BF16)],
        compiler_params=pltpu.CompilerParams(vmem_limit_bytes=24 * 2**20),
    )(place, *parts)


def pick(v, index, axis):
    return lax.dynamic_index_in_dim(v, index, axis, keepdims=False)


def add_up(parts):
    total = parts[0].astype(F32)
    for part in parts[1:]:
        total = total + part.astype(F32)
    return total


def body(
    hidden,
    queries,
    upstream,
    segment_ids,
    prompt_lengths,
    advantages,
    kv_weight,
    master,
    moment_one,
    moment_two,
):
    barrier = lax.optimization_barrier
    x, z, c = lax.axis_index("x"), lax.axis_index("z"), lax.axis_index("c")
    y = lax.axis_index(Y)
    length, width = hidden.shape
    rows = kv_weight.shape[0]
    cols = kv_weight.shape[1]
    segs = segment_ids[0]
    full_weight = lax.all_gather(kv_weight, ("yl", "z", "c"), axis=0, tiled=True)
    pos, live, adv_tok = token_terms(segs, prompt_lengths[0], advantages[0])
    local_count = jnp.sum(live.astype(F32))
    count = total_of(jnp.broadcast_to(local_count, (8, 128)))[0, 0]
    total_tokens = length * 256
    factor = F32(total_tokens) / jnp.maximum(count, F32(1.0))
    weight = jnp.where(live, adv_tok * factor, jnp.zeros_like(adv_tok))

    hidden_t = hidden.T.reshape(16, 2, rows, length)
    mine = pick(hidden_t, c, 1)
    theirs = shift(pick(hidden_t, 1 - c, 1), "c", 2, 1)
    hidden_pair = jnp.concatenate([mine, theirs], axis=-1).reshape(2, 8, rows, 2 * length)
    hz = jnp.transpose(hidden_pair[:, :, :RZ], (1, 0, 2, 3)).reshape(8, 2 * RZ, 2 * length)
    ha = hidden_pair[:, :, RZ:].reshape(16 * (rows - RZ), 2 * length)
    hidden, hz, ha = barrier((hidden, hz, ha))

    kv_pre = jnp.dot(hidden, full_weight, preferred_element_type=F32)
    query_grad, kv_grad = attention_backward(kv_pre, queries, upstream, pos, weight)
    pair = jnp.concatenate([kv_grad, shift(kv_grad, "c", 2, 1)], axis=0)

    sum_z = lax.psum_scatter(first_terms(hz, pair), "z", scatter_dimension=0, tiled=True)

    place = jnp.stack([x, y])

    out = barrier(tuple(terms(place, ha, pair)) + (kv_grad,))
    sent = tuple(shift(out[k], "x", 4, k) for k in (1, 2, 3))
    hidden_grad = hidden_gradient(out[4], full_weight)
    arrived = barrier(sent + (hidden_grad,))
    hidden_grad = arrived[3]
    out = turn(place, (out[0], *arrived[:3]))
    arrived = barrier(tuple(shift(out[k], Y, 4, k) for k in (1, 2, 3)))
    a = add_up([out[0], *arrived]).astype(BF16).reshape(2, 4, rows - RZ, HD)
    blocks = lax.all_to_all(sum_z.reshape(16, RZ, HD), ("x", *Y), 0, 0, tiled=True)
    theirs = swap(pick(a, 1 - z // 4, 0), "z", 8, 4)
    theirs, a, _ = barrier((theirs, a, sum_z))
    a = add_up([pick(a, z // 4, 0), theirs]).astype(BF16)
    sent = tuple(swap(pick(a, lax.rem(z, 4) ^ k, 0), "z", 8, k) for k in (1, 2, 3))
    arrived = barrier((blocks, *sent))
    summed = jnp.concatenate(
        [
            jnp.sum(arrived[0].astype(F32), axis=0),
            add_up([pick(a, lax.rem(z, 4), 0), *arrived[1:]]),
        ],
        axis=0,
    )
    weight_grad = summed / F32(total_tokens)
    new_moment_one = 0.9 * moment_one + 0.1 * weight_grad
    new_moment_two = 0.999 * moment_two + 0.001 * weight_grad * weight_grad
    first_hat = new_moment_one / (1.0 - 0.9**STEP)
    second_hat = new_moment_two / (1.0 - 0.999**STEP)
    new_master = master - 0.001 * (first_hat / (jnp.sqrt(second_hat) + 1e-08) + 0.1 * master)
    return (
        query_grad,
        hidden_grad,
        new_master,
        new_moment_one,
        new_moment_two,
    )


def solution(mesh):
    names = ("x", "yh", "yl", "z", "c")
    fine = Mesh(mesh.devices.reshape(4, 2, 2, 8, 2), names)
    tokens = P(names, None)
    state = P(("yl", "z", "c"), ("x", "yh"))
    return jax.shard_map(
        body,
        mesh=fine,
        in_specs=(tokens,) * 6 + (P(("yl", "z", "c"), None), state, state, state),
        out_specs=(tokens, tokens, state, state, state),
        check_vma=False,
    )
```

```python
import jax
import jax.numpy as jnp
from jax import lax
from jax.experimental import pallas as pl
from jax.experimental.pallas import tpu as pltpu
from jax.sharding import Mesh, PartitionSpec as P

HD = 128
STEP = 10
ROPE_BASE = 1000000.0
GROUP = 5
KVH = 4
SCALE = HD**-0.5
RZ = 96
Y = ("yh", "yl")
F32 = jnp.float32
BF16 = jnp.bfloat16
VMEM = pl.BlockSpec(memory_space=pltpu.VMEM)
SMEM = pl.BlockSpec(memory_space=pltpu.SMEM)


def positions_in_row(segs):
    length = segs.shape[0]
    index = jnp.arange(length, dtype=jnp.int32)
    previous = jnp.concatenate([segs[:1] - 1, segs[:-1]])
    starts = jnp.where(segs != previous, index, jnp.zeros_like(index))
    return index - lax.cummax(starts)


def token_terms(segs, prompts, advs):
    pos = positions_in_row(segs)
    onehot = segs[:, None] == jnp.arange(prompts.shape[0], dtype=jnp.int32)[None, :]
    prompt_tok = jnp.sum(
        jnp.where(onehot, prompts[None, :], jnp.zeros_like(prompts)[None, :]), axis=1
    )
    adv_tok = jnp.sum(jnp.where(onehot, advs[None, :], jnp.zeros_like(advs)[None, :]), axis=1)
    return (pos, pos >= prompt_tok, adv_tok)


def shift(v, axis, n, k):
    return lax.ppermute(v, axis, [(i, (i + k) % n) for i in range(n)])


def swap(v, axis, n, bit):
    return lax.ppermute(v, axis, [(i, i ^ bit) for i in range(n)])


def total_of(v):
    for axis, n, bit in (
        ("c", 2, 1), ("x", 4, 1), ("x", 4, 2), ("yl", 2, 1), ("yh", 2, 1),
        ("z", 8, 1), ("z", 8, 2), ("z", 8, 4),
    ):
        v = v + swap(v, axis, n, bit)
    return v


def dot_nt(a, b):
    return lax.dot_general(a, b, (((1,), (1,)), ((), ())), preferred_element_type=F32)


def dot_tn(a, b):
    return lax.dot_general(a, b, (((0,), (0,)), ((), ())), preferred_element_type=F32)


def attention_kernel(kpre, vpre, q, up, cos, sin, start, weight, qg, kvg):
    length = kpre.shape[0]
    half = length // 2
    cosine, sine = cos[...], sin[...]
    kp = kpre[...]
    k = (kp * cosine + pltpu.roll(kp, HD // 2, 1) * sine).astype(BF16)
    v = vpre[...].astype(BF16)
    dk, dv = [], []
    for part in range(2):
        rows, keys = slice(part * half, (part + 1) * half), (part + 1) * half
        kh, vh = k[:keys], v[:keys]
        key_index = lax.broadcasted_iota(jnp.int32, (keys, half), 0)
        query_index = lax.broadcasted_iota(jnp.int32, (keys, half), 1) + part * half
        allowed = (key_index >= start[:, rows]) & (key_index <= query_index)
        allowed = jnp.concatenate([allowed.astype(F32)] * GROUP, axis=1) > 0
        w = weight[rows, :]
        cols = [slice(g * HD, (g + 1) * HD) for g in range(GROUP)]
        qh = jnp.concatenate([q[rows, c] for c in cols], axis=0)
        do = jnp.concatenate([(up[rows, c].astype(F32) * w).astype(BF16) for c in cols], axis=0)
        s = jnp.where(allowed, dot_nt(kh, qh) * SCALE, F32(-1e30))
        e = jnp.exp(s - jnp.max(s, axis=0, keepdims=True))
        p = e * (1.0 / jnp.sum(e, axis=0, keepdims=True))
        low = p.astype(BF16)
        dp = dot_nt(vh, do)
        delta = jnp.sum(low.astype(F32) * dp, axis=0, keepdims=True)
        ds = (p * (dp - delta)).astype(BF16)
        dq = (dot_tn(ds, kh) * SCALE).astype(BF16)
        for g in range(GROUP):
            qg[rows, cols[g]] = dq[g * half : (g + 1) * half]
        dk.append(jnp.dot(ds, qh, preferred_element_type=F32))
        dv.append(jnp.dot(low, do, preferred_element_type=F32))
    dk = jnp.concatenate([dk[0] + dk[1][:half], dk[1][half:]], axis=0) * SCALE
    dv = jnp.concatenate([dv[0] + dv[1][:half], dv[1][half:]], axis=0)
    at = pl.multiple_of(pl.program_id(0) * HD, HD)
    kvg[:, pl.ds(at, HD)] = (dk * cosine - pltpu.roll(dk, HD // 2, 1) * sine).astype(BF16)
    kvg[:, pl.ds(at + KVH * HD, HD)] = dv.astype(BF16)


def attention_backward(kv_pre, queries, upstream, pos, weight):
    length = pos.shape[0]
    freq = ROPE_BASE ** (-(jnp.arange(HD // 2, dtype=F32) * 2.0 / HD))
    angle = pos.astype(F32)[:, None] * freq[None, :]
    cosine = jnp.concatenate([jnp.cos(angle), jnp.cos(angle)], axis=1)
    sine = jnp.concatenate([-jnp.sin(angle), jnp.sin(angle)], axis=1)
    start = (jnp.arange(length, dtype=jnp.int32) - pos)[None, :]
    whole = lambda shape: pl.BlockSpec(shape, lambda h: (0, 0))
    return pl.pallas_call(
        attention_kernel,
        grid=(KVH,),
        in_specs=[
            pl.BlockSpec((length, HD), lambda h: (0, h)),
            pl.BlockSpec((length, HD), lambda h: (0, h + KVH)),
            pl.BlockSpec((length, GROUP * HD), lambda h: (0, h)),
            pl.BlockSpec((length, GROUP * HD), lambda h: (0, h)),
            whole((length, HD)),
            whole((length, HD)),
            whole((1, length)),
            whole((length, 1)),
        ],
        out_specs=[
            pl.BlockSpec((length, GROUP * HD), lambda h: (0, h)),
            whole((length, 2 * KVH * HD)),
        ],
        out_shape=[
            jax.ShapeDtypeStruct((length, KVH * GROUP * HD), BF16),
            jax.ShapeDtypeStruct((length, 2 * KVH * HD), BF16),
        ],
        compiler_params=pltpu.CompilerParams(vmem_limit_bytes=32 * 2**20),
    )(kv_pre, kv_pre, queries, upstream, cosine, sine, start, weight[:, None])


def hidden_grad_kernel(kv, w, out):
    out[...] = dot_nt(kv[...], w[...]).astype(BF16)


def hidden_gradient(kv_grad, full_weight):
    length, cols = kv_grad.shape
    width = full_weight.shape[0]
    block = width // 8
    return pl.pallas_call(
        hidden_grad_kernel,
        grid=(8,),
        in_specs=[
            pl.BlockSpec((length, cols), lambda i: (0, 0)),
            pl.BlockSpec((block, cols), lambda i: (i, 0)),
        ],
        out_specs=pl.BlockSpec((length, block), lambda i: (0, i)),
        out_shape=jax.ShapeDtypeStruct((length, width), BF16),
        compiler_params=pltpu.CompilerParams(vmem_limit_bytes=48 * 2**20),
    )(kv_grad, full_weight)


def first_terms_kernel(h, pair, out):
    planes, rows, depth = 2, h.shape[1], h.shape[2]
    block = h[pl.ds(planes * pl.program_id(0), planes)].reshape(planes * rows, depth)
    term = jnp.dot(block, pair[...], preferred_element_type=F32).astype(BF16)
    for p in range(planes):
        for j in range(8):
            at = (8 * p + j) * rows
            out[at : at + rows, :] = term[p * rows : (p + 1) * rows, j * HD : (j + 1) * HD]


def first_terms(hz, pair):
    planes, rows, depth = hz.shape
    return pl.pallas_call(
        first_terms_kernel,
        grid=(planes // 2,),
        in_specs=[VMEM, VMEM],
        out_specs=pl.BlockSpec((16 * rows, HD), lambda i: (i, 0)),
        out_shape=jax.ShapeDtypeStruct((planes * 8 * rows, HD), BF16),
        compiler_params=pltpu.CompilerParams(vmem_limit_bytes=24 * 2**20),
    )(hz, pair)


def terms_kernel(place, ha, pair, *outs):
    for k in range(4):
        at = pl.multiple_of(lax.rem(place[0] + k, 4) * 2 * HD, 2 * HD)
        cols = pair[:, pl.ds(at, 2 * HD)]
        outs[k][...] = jnp.dot(ha[...], cols, preferred_element_type=F32).astype(BF16)


def terms(place, ha, pair):
    return pl.pallas_call(
        terms_kernel,
        in_specs=[SMEM, VMEM, VMEM],
        out_specs=[VMEM] * 4,
        out_shape=[jax.ShapeDtypeStruct((ha.shape[0], 2 * HD), BF16)] * 4,
        compiler_params=pltpu.CompilerParams(vmem_limit_bytes=24 * 2**20),
    )(place, ha, pair)


def turn_kernel(place, *refs):
    parts, outs, total = refs[:4], refs[4:8], refs[8]
    total[...] = add_up([r[...] for r in parts]).astype(BF16)
    half = total.shape[0] // 2
    for k in range(4):
        there = lax.rem(place[1] + k, 4)
        row = pl.multiple_of(lax.rem(there, 2) * half, half)
        col = pl.multiple_of(lax.div(there, 2) * HD, HD)
        outs[k][...] = total[pl.ds(row, half), pl.ds(col, HD)]


def turn(place, parts):
    rows = parts[0].shape[0]
    return pl.pallas_call(
        turn_kernel,
        in_specs=[SMEM] + [VMEM] * 4,
        out_specs=[VMEM] * 4,
        out_shape=[jax.ShapeDtypeStruct((rows // 2, HD), BF16)] * 4,
        scratch_shapes=[pltpu.VMEM(parts[0].shape, BF16)],
        compiler_params=pltpu.CompilerParams(vmem_limit_bytes=24 * 2**20),
    )(place, *parts)


def pick(v, index, axis):
    return lax.dynamic_index_in_dim(v, index, axis, keepdims=False)


def add_up(parts):
    total = parts[0].astype(F32)
    for part in parts[1:]:
        total = total + part.astype(F32)
    return total


def body(
    hidden,
    queries,
    upstream,
    segment_ids,
    prompt_lengths,
    advantages,
    kv_weight,
    master,
    moment_one,
    moment_two,
):
    barrier = lax.optimization_barrier
    x, z, c = lax.axis_index("x"), lax.axis_index("z"), lax.axis_index("c")
    y = lax.axis_index(Y)
    length, width = hidden.shape
    rows = kv_weight.shape[0]
    cols = kv_weight.shape[1]
    segs = segment_ids[0]
    full_weight = lax.all_gather(kv_weight, ("yl", "z", "c"), axis=0, tiled=True)
    pos, live, adv_tok = token_terms(segs, prompt_lengths[0], advantages[0])
    local_count = jnp.sum(live.astype(F32))
    count = total_of(jnp.broadcast_to(local_count, (8, 128)))[0, 0]
    total_tokens = length * 256
    factor = F32(total_tokens) / jnp.maximum(count, F32(1.0))
    weight = jnp.where(live, adv_tok * factor, jnp.zeros_like(adv_tok))

    hidden_t = hidden.T.reshape(16, 2, rows, length)
    mine = pick(hidden_t, c, 1)
    theirs = shift(pick(hidden_t, 1 - c, 1), "c", 2, 1)
    hidden_pair = jnp.concatenate([mine, theirs], axis=-1).reshape(2, 8, rows, 2 * length)
    hz = jnp.transpose(hidden_pair[:, :, :RZ], (1, 0, 2, 3)).reshape(8, 2 * RZ, 2 * length)
    ha = hidden_pair[:, :, RZ:].reshape(16 * (rows - RZ), 2 * length)
    hidden, hz, ha = barrier((hidden, hz, ha))

    kv_pre = jnp.dot(hidden, full_weight, preferred_element_type=F32)
    query_grad, kv_grad = attention_backward(kv_pre, queries, upstream, pos, weight)
    pair = jnp.concatenate([kv_grad, shift(kv_grad, "c", 2, 1)], axis=0)

    sum_z = lax.psum_scatter(first_terms(hz, pair), "z", scatter_dimension=0, tiled=True)

    place = jnp.stack([x, y])

    out = barrier(tuple(terms(place, ha, pair)) + (kv_grad,))
    sent = tuple(shift(out[k], "x", 4, k) for k in (1, 2, 3))
    hidden_grad = hidden_gradient(out[4], full_weight)
    arrived = barrier(sent + (hidden_grad,))
    hidden_grad = arrived[3]
    out = turn(place, (out[0], *arrived[:3]))
    arrived = barrier(tuple(shift(out[k], Y, 4, k) for k in (1, 2, 3)))
    a = add_up([out[0], *arrived]).astype(BF16).reshape(2, 4, rows - RZ, HD)
    blocks = lax.all_to_all(sum_z.reshape(16, RZ, HD), ("x", *Y), 0, 0, tiled=True)
    near = lax.rem(z, 4)
    theirs = tuple(swap(pick(a, near ^ k, 1), "z", 8, k) for k in (1, 2, 3))
    theirs, a, _ = barrier((theirs, a, sum_z))
    a = add_up([pick(a, near, 1), *theirs]).astype(BF16)
    blocks, far = barrier((blocks, swap(pick(a, 1 - z // 4, 0), "z", 8, 4)))
    summed = jnp.concatenate(
        [jnp.sum(blocks.astype(F32), axis=0), add_up([pick(a, z // 4, 0), far])], axis=0
    )
    weight_grad = summed / F32(total_tokens)
    new_moment_one = 0.9 * moment_one + 0.1 * weight_grad
    new_moment_two = 0.999 * moment_two + 0.001 * weight_grad * weight_grad
    first_hat = new_moment_one / (1.0 - 0.9**STEP)
    second_hat = new_moment_two / (1.0 - 0.999**STEP)
    new_master = master - 0.001 * (first_hat / (jnp.sqrt(second_hat) + 1e-08) + 0.1 * master)
    return (
        query_grad,
        hidden_grad,
        new_master,
        new_moment_one,
        new_moment_two,
    )


def solution(mesh):
    names = ("x", "yh", "yl", "z", "c")
    fine = Mesh(mesh.devices.reshape(4, 2, 2, 8, 2), names)
    tokens = P(names, None)
    state = P(("yl", "z", "c"), ("x", "yh"))
    return jax.shard_map(
        body,
        mesh=fine,
        in_specs=(tokens,) * 6 + (P(("yl", "z", "c"), None), state, state, state),
        out_specs=(tokens, tokens, state, state, state),
        check_vma=False,
    )
```
